256 devices in a mesh: slab: 64 (over y_hi, x, z), mp: 4 (over y_lo, core).
Axes of the slice: x: 4, y: 4 (y_hi: 2, y_lo: 2; y = y_hi * 2 + y_lo), z: 8, core: 2. Of those that a mesh axis runs over, the one named last changes fastest.
Arguments:
- query_emb: bfloat16 [16384, 1024], P('slab', 'mp'), may hold values from -6 to 6
- passage_emb: bfloat16 [32768, 1024], P('slab', 'mp'), may hold values from -6 to 6
- head: bfloat16 [1024, 1024], P('mp'), may hold values from -0.1875 to 0.1875
- fn_mask: int32 [16384, 5, 4], P('slab'), may hold values 0 or 1
- counts: int32 [64], replicated, may hold values from 1 to 512, 24576 in all
- positive_slot: int32 [16384], P('slab'), may hold values from 0 to 511
- query_weight: float32 [16384], P('slab'), may hold values from 0.5 to 2
Outputs:
- query_grad: bfloat16 [16384, 1024], P('slab', 'mp')
- passage_grad: bfloat16 [32768, 1024], P('slab', 'mp')
- head_grad: float32 [1024, 1024], P('mp')
The draws below stay inside these ranges and needn't reach their ends.
Inputs may be any that keep to these rules, and one draw needn't show every extreme that they name: `counts`: the largest count is 512.
All inputs are finite; a program needn't handle non-finite values. No bound on the sum of `fn_mask` on one device may be relied on, other than what follows from the above.
Results may differ from the reference program's by a relative error of at most 0.034.
Values may be sent and summed in bfloat16 or wider, within the bound.
A program may use at most 64 MiB of HBM per device.

```python
import math
import jax
import jax.numpy as jnp
import numpy as np
from jax import lax

D = 1024
Q_DEV = 256
P_DEV = 512
TILE = 128
BAND = 5
TILES = 4
SLABS = 64
WBLK = 256
QUERIES = 16384
PASSAGES = 32768
N_MP = 4


def with_ends(entries, key, least, high):
    dims = entries.shape
    index_at = [jax.random.randint(jax.random.fold_in(key, axis), (), 0, dims[axis]) for axis in range(len(dims))]
    entries = entries.at[tuple(index_at)].set(least)
    longest = dims.index(max(dims))
    index_at[longest] = (index_at[longest] + 1) % dims[longest]
    return entries.at[tuple(index_at)].set(high)


def level_of(rng, extent, pieces, least, largest):
    level = 1.0
    for position, parts in pieces:
        draws = jax.random.uniform(jax.random.fold_in(jax.random.fold_in(rng, 6), position), (parts,), jnp.float32, least / len(pieces), largest / len(pieces))
        level = level * jnp.repeat(jnp.exp(draws), extent[position] // parts).reshape((-1,) + (1,) * (len(extent) - 1 - position))
    return level


def length_profile(number_of, total, most, slope):
    loads = [(1 << 20) // math.isqrt(standing ** slope) + 1 for standing in range(2, number_of + 1)]
    surplus, given = total - most - (number_of - 1), [1] * (number_of - 1)
    while surplus > 0:
        candidates = [i for i in range(number_of - 1) if given[i] < most]
        pool, remaining = sum([loads[i] for i in candidates]), surplus
        for i in candidates:
            more = min(most - given[i], max(1, remaining * loads[i] // pool), surplus)
            given[i] = given[i] + more
            surplus = surplus - more
    return np.array([most] + given)


def uneven_parts(own_key, number_of, total, bound, lean):
    if number_of == 2:
        one = jax.random.randint(own_key, (), max(1, total - bound), min(bound, total - 1) + 1)
        return jnp.stack([one, total - one])
    sizes = jnp.asarray(length_profile(number_of, total, bound, lean), jnp.int32)
    couples = (number_of - 1) // 2
    giver, taker = sizes[1:1 + 2 * couples:2], sizes[2:2 + 2 * couples:2]
    slack = jnp.minimum(giver - 1, bound - taker)
    passed = jax.random.randint(jax.random.fold_in(own_key, 1), (couples,), 0, 1 << 20) % (slack + 1)
    sizes = sizes.at[1:1 + 2 * couples:2].set(giver - passed).at[2:2 + 2 * couples:2].set(taker + passed)
    return sizes[jax.random.permutation(jax.random.fold_in(own_key, 2), number_of)]


def noise(key, shape, deviation, most, split=(), held_as=jnp.bfloat16):
    array = deviation * jax.random.normal(key, shape, jnp.float32)
    if split:
        array = array * level_of(key, shape, split, -0.22, 0.18)
    return jnp.clip(array, -most, most).astype(held_as)


def setup_inputs(seed: int = 0) -> dict:
    arg_keys = jax.random.split(jax.random.key(seed), 8)
    return {
        "query_emb": noise(arg_keys[0], (QUERIES, D), 1.0, 6.0, ((0, 64), (1, 4))),
        "passage_emb": noise(arg_keys[1], (PASSAGES, D), 1.0, 6.0, ((0, 64), (1, 4))),
        "head": noise(arg_keys[2], (D, D), D ** -0.5, 0.1875, ((0, 4),)),
        "fn_mask": with_ends((jax.random.randint(arg_keys[3], (QUERIES, BAND, TILES), 0, 4) < 3).astype(jnp.int32), jax.random.fold_in(arg_keys[3], 1), 0, 1),
        "counts": uneven_parts(arg_keys[4], SLABS, SLABS * P_DEV * 3 // 4, P_DEV, 2).astype(jnp.int32),
        "positive_slot": with_ends(jax.random.randint(arg_keys[5], (QUERIES,), 0, P_DEV), jax.random.fold_in(arg_keys[5], 1), 0, P_DEV - 1).astype(jnp.int32),
        "query_weight": jnp.clip(jnp.exp(math.log(2.0) - 1.3862944 * jax.random.uniform(arg_keys[6], (QUERIES,), jnp.float32) ** level_of(arg_keys[6], (QUERIES,), ((0, 64),), -0.2, 0.2)), 0.5, 2.0),
    }


EPS = 1e-06
TAU = 0.05

def project(embedding, head):
    total = jnp.zeros((embedding.shape[0], head.shape[1]), jnp.float32)
    for block_id in range(N_MP):
        start_row = block_id * WBLK
        partial_value = jnp.dot(embedding[:, start_row:start_row + WBLK], head[start_row:start_row + WBLK], preferred_element_type=jnp.float32)
        partial_value = lax.optimization_barrier(partial_value.astype(jnp.bfloat16))
        total = total + partial_value.astype(jnp.float32)
    return total

def reference(query_emb, passage_emb, head, fn_mask, counts, positive_slot, query_weight):
    stacked = jnp.concatenate([query_emb, passage_emb], axis=0)
    projected = project(stacked, head)
    row_norms = jnp.sqrt(lax.optimization_barrier(jnp.sum(projected * projected, axis=1, keepdims=True)) + EPS)
    unit_rows = projected / row_norms
    unit_half = unit_rows.astype(jnp.bfloat16)
    queries = query_emb.shape[0]
    query_units = unit_half[:queries]
    zero_slabs = jnp.zeros((2 * P_DEV, D), jnp.bfloat16)
    padded_units = jnp.concatenate([zero_slabs, unit_half[queries:], zero_slabs], axis=0)
    padded_counts = jnp.concatenate([jnp.zeros((2,), jnp.int32), counts, jnp.zeros((2,), jnp.int32)])
    slot_ids = jnp.arange(P_DEV, dtype=jnp.int32)
    centre = (jnp.arange(BAND, dtype=jnp.int32) == BAND // 2)[:, None]

    def slab_step(accum, slab_index):
        own_queries = lax.dynamic_slice_in_dim(query_units, slab_index * Q_DEV, Q_DEV, 0)
        band_units = lax.dynamic_slice_in_dim(padded_units, slab_index * P_DEV, BAND * P_DEV, 0)
        near_counts = lax.dynamic_slice_in_dim(padded_counts, slab_index, BAND, 0)
        mask_rows = lax.dynamic_slice_in_dim(fn_mask, slab_index * Q_DEV, Q_DEV, 0)
        mask_cols = jnp.repeat(mask_rows, TILE, axis=2)
        wanted = lax.dynamic_slice_in_dim(positive_slot, slab_index * Q_DEV, Q_DEV, 0) % near_counts[BAND // 2]
        weights = lax.dynamic_slice_in_dim(query_weight, slab_index * Q_DEV, Q_DEV, 0)
        scores = lax.dot_general(own_queries, band_units, (((1,), (1,)), ((), ())), preferred_element_type=jnp.float32) / TAU
        scores = scores.reshape(Q_DEV, BAND, P_DEV)
        inside = slot_ids[None, :] < near_counts[:, None]
        is_positive = centre[None] & (slot_ids[None, None, :] == wanted[:, None, None])
        kept = inside[None] & ((mask_cols == 1) | is_positive)
        exp_terms = jnp.where(kept, jnp.exp(scores), jnp.zeros_like(scores))
        totals = lax.optimization_barrier(jnp.sum(exp_terms, axis=(1, 2)))
        probability = exp_terms / totals[:, None, None]
        coefficient = (weights[:, None, None] * (probability - is_positive.astype(jnp.float32)) / TAU).astype(jnp.bfloat16)
        coefficient = coefficient.reshape(Q_DEV, BAND * P_DEV)
        query_part = jnp.dot(coefficient, band_units, preferred_element_type=jnp.float32)
        passage_part = lax.dot_general(coefficient, own_queries, (((0,), (0,)), ((), ())), preferred_element_type=jnp.float32)
        previous = lax.dynamic_slice_in_dim(accum, slab_index * P_DEV, BAND * P_DEV, 0)
        accum = lax.dynamic_update_slice_in_dim(accum, previous + passage_part, slab_index * P_DEV, 0)
        return (accum, query_part)
    start_accum = jnp.zeros(((SLABS + 4) * P_DEV, D), jnp.float32)
    accum, query_parts = lax.scan(slab_step, start_accum, jnp.arange(SLABS, dtype=jnp.int32))
    passage_parts = accum[2 * P_DEV:2 * P_DEV + SLABS * P_DEV]
    summed = jnp.concatenate([query_parts.reshape(queries, D), passage_parts], axis=0)
    radial = lax.optimization_barrier(jnp.sum(unit_rows * summed, axis=1, keepdims=True))
    grad_proj = ((summed - unit_rows * radial) / row_norms).astype(jnp.bfloat16)
    emb_grad = jnp.dot(grad_proj, head.T, preferred_element_type=jnp.float32).astype(jnp.bfloat16)
    head_grad = lax.dot_general(stacked, grad_proj, (((0,), (0,)), ((), ())), preferred_element_type=jnp.float32)
    return (emb_grad[:queries], emb_grad[queries:], head_grad)
```

```python
import jax
import jax.numpy as jnp
from jax import lax
from jax.experimental import pallas as pl
from jax.experimental.pallas import tpu as pltpu
from jax.sharding import PartitionSpec as P

EPS = 1e-06
TAU = 0.05
D = 1024
QM = 64
PM = 128
NQ = 5 * QM
SEMS = 96
MESH = pl.DeviceIdType.MESH
BF = jnp.bfloat16
F32 = jnp.float32


def kernel(
    q_ref, p_ref, head_ref, mask_ref, counts_ref, pos_ref, weight_ref,
    oq_ref, op_ref, oh_ref,
    part_q, part_p, rq, rp, yq, yp, zq, zp,
    unit_q, unit_p, norm_q, norm_p,
    qb, pb, auxs, auxr, auxc, ef, eb, tts, ttr, gs, gr,
    pps, ppf, pr, py, pz, pgq, pgp,
    hf, hb, ax, bz, a1, b1, az, bx, a1f, b1f, c2, cr, ga, gb, gaf, gbf,
    ssem, rsem,
):
    slab = lax.axis_index("slab")
    m = lax.axis_index("mp")
    core, low = m % 2, m // 2
    sib = 2 * low + 1 - core
    opp = 2 * (1 - low) + core
    osib = 2 * (1 - low) + 1 - core
    high, xi, zi = slab // 32, (slab // 8) % 4, slab % 8

    def at_slab(distance):
        return ((slab + distance + 64) % 64, m)

    def at_x(step):
        return (high * 32 + ((xi + step) % 4) * 8 + zi, m)

    def at_z(step):
        return (high * 32 + xi * 8 + (zi + step) % 8, m)

    to_sib, to_opp, to_high = (slab, sib), (slab, opp), ((slab + 32) % 64, m)
    peers = [to_sib, to_opp, to_high]
    peers += [at_slab(k) for k in (-4, -3, -2, -1, 1, 2, 3, 4)]
    peers += [at_x(k) for k in range(1, 4)] + [at_z(k) for k in range(1, 8)]
    used = [0]

    def send(src, dst, device):
        i = used[0]
        used[0] += 1
        copy = pltpu.make_async_remote_copy(
            src_ref=src, dst_ref=dst, send_sem=ssem.at[i], recv_sem=rsem.at[i],
            device_id=device, device_id_type=MESH,
        )
        copy.start()
        sent.append(copy)
        return copy

    sent = []

    def rows(count, index):
        return pl.ds(pl.multiple_of(count * index, count), count)

    barrier = pltpu.get_barrier_semaphore()
    for peer in peers:
        pl.semaphore_signal(barrier, inc=1, device_id=peer, device_id_type=MESH)

    part_q[...] = jnp.dot(q_ref[...], head_ref[...], preferred_element_type=F32).astype(BF)
    pl.semaphore_wait(barrier, len(peers))
    q1 = send(part_q.at[rows(QM, osib)], rq.at[1], to_sib)
    q0 = send(part_q.at[rows(QM, sib)], rq.at[0], to_sib)
    part_p[...] = jnp.dot(p_ref[...], head_ref[...], preferred_element_type=F32).astype(BF)
    p1 = send(part_p.at[rows(PM, osib)], rp.at[1], to_sib)
    p0 = send(part_p.at[rows(PM, sib)], rp.at[0], to_sib)
    q1.wait_recv()
    yq[...] = (part_q[rows(QM, opp)].astype(F32) + rq[1].astype(F32)).astype(BF)
    q2 = send(yq, zq, to_opp)
    p1.wait_recv()
    yp[...] = (part_p[rows(PM, opp)].astype(F32) + rp[1].astype(F32)).astype(BF)
    p2 = send(yp, zp, to_opp)

    def own_lanes(value):
        quarters = [value[:, k * QM : (k + 1) * QM] for k in range(4)]
        return jnp.where(
            m == 0, quarters[0],
            jnp.where(m == 1, quarters[1], jnp.where(m == 2, quarters[2], quarters[3])),
        )

    count = counts_ref[slab]
    count_f = count.astype(F32)
    weight = own_lanes(weight_ref[...])
    slot = own_lanes(pos_ref[...].astype(F32))
    wanted = slot - count_f * jnp.floor((slot + 0.5) / count_f)
    auxs[...] = jnp.zeros_like(auxs)
    for k in range(5):
        auxs[k, 0:4, 0:QM] = own_lanes(mask_ref[k].astype(F32))
        auxs[k, 4:5, 0:QM] = weight

    def normalise(projected):
        norm = jnp.sqrt(jnp.sum(projected * projected, axis=1, keepdims=True) + EPS)
        return projected / norm, norm

    q0.wait_recv()
    q2.wait_recv()
    unit, norm = normalise(
        part_q[rows(QM, m)].astype(F32) + rq[0].astype(F32) + zq[...].astype(F32)
    )
    unit_q[...] = unit
    norm_q[...] = norm
    qb[2 * QM : 3 * QM] = unit.astype(BF)
    queries, auxes = [], []
    for k in (1, -1, 2, -2):
        queries.append(
            send(qb.at[2 * QM : 3 * QM], qb.at[(2 - k) * QM : (3 - k) * QM], at_slab(k))
        )
        auxes.append(send(auxs.at[2 + k], auxr.at[2 - k], at_slab(k)))

    p0.wait_recv()
    p2.wait_recv()
    unit, norm = normalise(
        part_p[rows(PM, m)].astype(F32) + rp[0].astype(F32) + zp[...].astype(F32)
    )
    unit_p[...] = unit
    norm_p[...] = norm
    pb[rows(PM, m)] = unit.astype(BF)

    def gather(ref, size):
        mine = ref.at[rows(size, m)]
        over = send(mine, mine, to_opp)
        near = send(mine, mine, to_sib)
        over.wait_recv()
        theirs = ref.at[rows(size, opp)]
        far = send(theirs, theirs, to_sib)
        near.wait_recv()
        far.wait_recv()

    gather(pb, PM)
    for copy in queries + auxes:
        copy.wait_recv()

    auxr[2] = auxs[2]
    for k in range(5):
        auxc[:, k * QM : (k + 1) * QM] = auxr[k][:, 0:QM]
        here = slab + (k - 2)
        real = jnp.where(here >= 0, jnp.where(here < 64, 1.0, 0.0), 0.0).astype(F32)
        auxc[0:4, k * QM : (k + 1) * QM] = auxr[k][0:4, 0:QM] * real
        auxc[5:6, k * QM : (k + 1) * QM] = wanted if k == 2 else jnp.full((1, QM), -1.0, F32)
    scores = lax.dot_general(
        pb[...], qb[...], (((1,), (1,)), ((), ())), preferred_element_type=F32
    )
    slot_ids = lax.broadcasted_iota(jnp.int32, (PM, NQ), 0)
    others = jnp.zeros((1, NQ), F32)
    positive = jnp.zeros((1, NQ), F32)
    for tile in range(4):
        ids = slot_ids + tile * PM
        is_positive = ids.astype(F32) == auxc[5:6, :]
        kept = (ids < count) & (auxc[tile : tile + 1, :] > 0.5) & jnp.logical_not(is_positive)
        grown = jnp.exp(scores[tile * PM : (tile + 1) * PM] / TAU)
        terms = jnp.where(kept, grown, 0.0)
        others = others + jnp.sum(terms, axis=0, keepdims=True)
        positive = positive + jnp.sum(jnp.where(is_positive, grown, 0.0), axis=0, keepdims=True)
        ef[tile * PM : (tile + 1) * PM] = terms
        eb[tile * PM : (tile + 1) * PM] = terms.astype(BF)
    tts[...] = jnp.zeros_like(tts)
    tts[0:1, 0:NQ] = others
    tts[1:2, 0:NQ] = positive
    totals = [send(tts, ttr.at[4 - k], at_slab(k)) for k in (1, -1, 2, -2, 3, -3, 4, -4)]

    terms = lax.dot_general(
        eb[...], pb[...], (((0,), (0,)), ((), ())), preferred_element_type=F32
    )
    returns = []
    for k in (2, -2, 1, -1):
        gs[2 + k] = terms[(2 + k) * QM : (3 + k) * QM].astype(BF)
        returns.append(send(gs.at[2 + k], gr.at[2 - k], at_slab(k)))
    own_terms = terms[2 * QM : 3 * QM]

    ttr[4] = tts[...]
    for copy in totals:
        copy.wait_recv()
    for k in range(-2, 3):
        rest = jnp.zeros((1, QM), F32)
        for j in range(-2, 3):
            rest = rest + ttr[k + j + 4][0:1, (2 - j) * QM : (3 - j) * QM]
        whole = rest + ttr[k + 4][1:2, 2 * QM : 3 * QM]
        lanes = slice((2 + k) * QM, (3 + k) * QM)
        auxc[6:7, lanes] = auxc[4:5, lanes] / (whole * TAU)
        if k == 0:
            own_rest, own_whole = rest, whole
            auxc[7:8, lanes] = auxc[6:7, lanes] * rest
        else:
            auxc[7:8, lanes] = jnp.zeros((1, QM), F32)

    for tile in range(4):
        here = slice(tile * PM, (tile + 1) * PM)
        is_positive = (slot_ids + tile * PM).astype(F32) == auxc[5:6, :]
        coefficient = jnp.where(is_positive, -auxc[7:8, :], ef[here] * auxc[6:7, :])
        part = jnp.dot(coefficient.astype(BF), qb[...], preferred_element_type=F32)
        ppf[here] = part
        pps[here] = part.astype(BF)
    p1 = send(pps.at[rows(PM, osib)], pr.at[1], to_sib)
    p0 = send(pps.at[rows(PM, sib)], pr.at[0], to_sib)
    p1.wait_recv()
    py[...] = (ppf[rows(PM, opp)] + pr[1].astype(F32)).astype(BF)
    p2 = send(py, pz, to_opp)

    def tangent(unit, norm, grad):
        radial = jnp.sum(unit * grad, axis=1, keepdims=True)
        return ((grad - unit * radial) / norm).astype(BF)

    eye = lax.broadcasted_iota(jnp.int32, (QM, QM), 0) == lax.broadcasted_iota(
        jnp.int32, (QM, QM), 1
    )

    def column(row):
        return jnp.sum(jnp.where(eye, row, 0.0), axis=1, keepdims=True)

    one_hot = (
        lax.broadcasted_iota(jnp.int32, (4 * PM, QM), 0).astype(F32) == wanted
    ).astype(F32).astype(BF)
    chosen = lax.dot_general(
        one_hot, pb[...], (((0,), (0,)), ((), ())), preferred_element_type=F32
    )
    scale = column(weight / (own_whole * TAU))
    drop = column(weight * own_rest / (own_whole * TAU))
    for copy in returns:
        copy.wait_recv()
    for k in (0, 1, 3, 4):
        own_terms = own_terms + gr[k].astype(F32)
    pgq[rows(QM, m)] = tangent(unit_q[...], norm_q[...], own_terms * scale - chosen * drop)
    gather(pgq, QM)
    p0.wait_recv()
    p2.wait_recv()
    summed = ppf[rows(PM, m)] + pr[0].astype(F32) + pz[...].astype(F32)
    pgp[rows(PM, m)] = tangent(unit_p[...], norm_p[...], summed)
    gather(pgp, PM)

    across = (((0,), (0,)), ((), ()))
    term = lax.dot_general(
        q_ref[...], pgq[...], across, preferred_element_type=F32
    ) + lax.dot_general(p_ref[...], pgp[...], across, preferred_element_type=F32)
    hf[...] = term
    hb[...] = term.astype(BF)

    def cols(index):
        return pl.ds(pl.multiple_of(index * 128, 128), 128)

    first = []
    for k in (2, 1, 3):
        first.append(send(hb.at[rows(48, (xi + k) % 4)], ax.at[k - 1], at_x(k)))
    for k in (4, 3, 5, 2, 6, 1, 7):
        first.append(send(hb.at[192:256, cols((zi + k) % 8)], bz.at[k - 1], at_z(k)))

    back = (((1,), (1,)), ((), ()))
    oq_ref[...] = lax.dot_general(
        pgq[...], head_ref[...], back, preferred_element_type=F32
    ).astype(BF)
    op_ref[...] = lax.dot_general(
        pgp[...], head_ref[...], back, preferred_element_type=F32
    ).astype(BF)

    for copy in first:
        copy.wait_recv()
    total = hf[rows(48, xi)]
    for k in range(3):
        total = total + ax[k].astype(F32)
    a1f[...] = total
    a1[...] = total.astype(BF)
    total = hf[192:256, cols(zi)]
    for k in range(7):
        total = total + bz[k].astype(F32)
    b1f[...] = total
    b1[...] = total.astype(BF)
    second = []
    for k in (4, 3, 5, 2, 6, 1, 7):
        second.append(send(a1.at[:, cols((zi + k) % 8)], az.at[k - 1], at_z(k)))
    for k in (2, 1, 3):
        second.append(send(b1.at[rows(16, (xi + k) % 4)], bx.at[k - 1], at_x(k)))
    for copy in second:
        copy.wait_recv()
    total = a1f[:, cols(zi)]
    for k in range(7):
        total = total + az[k].astype(F32)
    c2[0:48] = total.astype(BF)
    total = b1f[rows(16, xi)]
    for k in range(3):
        total = total + bx[k].astype(F32)
    c2[48:64] = total.astype(BF)
    send(c2, cr, to_high).wait_recv()
    final = (c2[...].astype(F32) + cr[...].astype(F32)).astype(BF)
    ga[:, cols(zi)] = final[0:48]
    gb[rows(16, xi)] = final[48:64]
    third = []
    for k in (4, 3, 5, 2, 6, 1, 7):
        third.append(send(ga.at[:, cols(zi)], ga.at[:, cols(zi)], at_z(k)))
    fourth = []
    for k in (2, 1, 3):
        fourth.append(send(gb.at[rows(16, xi)], gb.at[rows(16, xi)], at_x(k)))
    for copy in fourth:
        copy.wait_recv()
    last = []
    for k in (4, 3, 5, 2, 6, 1, 7):
        last.append(send(gb, gbf.at[:, cols(zi)], at_z(k)))
    for copy in third:
        copy.wait_recv()
    for k in (2, 1, 3):
        last.append(send(ga, gaf.at[rows(48, xi)], at_x(k)))
    gaf[rows(48, xi)] = ga[...]
    gbf[:, cols(zi)] = gb[...]
    for copy in last:
        copy.wait_recv()
    oh_ref[0:192] = gaf[...].astype(F32)
    oh_ref[192:256] = gbf[...].astype(F32)
    for copy in sent:
        copy.wait_send()


def body(query_emb, passage_emb, head, fn_mask, counts, positive_slot, query_weight):
    vmem = pl.BlockSpec(memory_space=pltpu.VMEM)
    smem = pl.BlockSpec(memory_space=pltpu.SMEM)

    def half(*shape):
        return pltpu.VMEM(shape, BF)

    def full(*shape):
        return pltpu.VMEM(shape, F32)

    return pl.pallas_call(
        kernel,
        out_shape=(
            jax.ShapeDtypeStruct((256, 256), BF),
            jax.ShapeDtypeStruct((512, 256), BF),
            jax.ShapeDtypeStruct((256, D), F32),
        ),
        in_specs=[vmem, vmem, vmem, vmem, smem, vmem, vmem],
        out_specs=(vmem, vmem, vmem),
        scratch_shapes=[
            half(256, D), half(512, D), half(2, QM, D), half(2, PM, D),
            half(QM, D), half(PM, D), half(QM, D), half(PM, D),
            full(QM, D), full(PM, D), full(QM, 1), full(PM, 1),
            half(NQ, D), half(4 * PM, D), full(5, 8, 128), full(5, 8, 128), full(8, NQ),
            full(4 * PM, NQ), half(4 * PM, NQ), full(8, 384), full(9, 8, 384),
            half(5, QM, D), half(5, QM, D),
            half(512, D), full(512, D), half(2, PM, D), half(PM, D), half(PM, D),
            half(256, D), half(512, D),
            full(256, D), half(256, D), half(3, 48, D), half(7, 64, 128),
            half(48, D), half(64, 128), half(7, 48, 128), half(3, 16, 128),
            full(48, D), full(64, 128), half(64, 128), half(64, 128),
            half(48, D), half(64, 128), half(192, D), half(64, D),
            pltpu.SemaphoreType.DMA((SEMS,)), pltpu.SemaphoreType.DMA((SEMS,)),
        ],
        compiler_params=pltpu.CompilerParams(
            collective_id=0, has_side_effects=True, vmem_limit_bytes=48 << 20
        ),
        cost_estimate=pl.CostEstimate(flops=3 << 30, bytes_accessed=4 << 20, transcendentals=0),
    )(
        query_emb, passage_emb, head, jnp.transpose(fn_mask, (1, 2, 0)), counts,
        positive_slot.reshape(1, -1), query_weight.reshape(1, -1),
    )


def solution(mesh):
    return jax.shard_map(
        body,
        mesh=mesh,
        in_specs=(
            P("slab", "mp"), P("slab", "mp"), P("mp", None), P("slab", None, None),
            P(), P("slab"), P("slab"),
        ),
        out_specs=(P("slab", "mp"), P("slab", "mp"), P("mp", None)),
        check_vma=False,
    )
```

```python
import jax
import jax.numpy as jnp
from jax import lax
from jax.experimental import pallas as pl
from jax.experimental.pallas import tpu as pltpu
from jax.sharding import PartitionSpec as P

EPS = 1e-06
TAU = 0.05
D = 1024
QM = 64
PM = 128
NQ = 5 * QM
SEMS = 112
MESH = pl.DeviceIdType.MESH
BF = jnp.bfloat16
F32 = jnp.float32


def kernel(
    q_hbm, p_hbm, head_hbm, mask_hbm, counts_ref, pos_hbm, weight_hbm,
    oq_ref, op_ref, oh_ref,
    q_ref, p_ref, head, mask_ref, pos_ref, weight_ref,
    part_q, part_p, rq, rp, yq, yp, zq, zp,
    unit_q, unit_p, norm_q, norm_p,
    qb, pb, auxs, auxr, auxc, ef, eb, tts, ttr, gs, gr,
    pps, ppf, pr, py, pz, xo, pgo, eo,
    tsend, trecv, hf, hb, ax, cy, a1f, c1f, a1, c1, ay, cx, e1f, e1, ez, gz,
    lsem, ssem, rsem,
):
    slab = lax.axis_index("slab")
    m = lax.axis_index("mp")
    core, low = m % 2, m // 2
    sib = 2 * low + 1 - core
    opp = 2 * (1 - low) + core
    osib = 2 * (1 - low) + 1 - core
    high, xi, zi = slab // 32, (slab // 8) % 4, slab % 8

    def at_slab(distance):
        there = (slab + distance + 64) % 64
        return (there, jnp.where(there // 32 == high, m, opp))

    def at_x(step):
        return (high * 32 + ((xi + step) % 4) * 8 + zi, m)

    def at_z(step):
        return (high * 32 + xi * 8 + (zi + step) % 8, m)

    def inside(distance):
        return jnp.logical_and(slab + distance >= 0, slab + distance < 64)

    to_sib, to_opp, to_osib = (slab, sib), (slab, opp), (slab, osib)
    to_high, to_back = ((slab + 32) % 64, m), ((slab + 32) % 64, opp)
    peers = [to_sib, to_opp, to_osib, to_high, to_back]
    peers += [at_slab(k) for k in (-4, -3, -2, -1, 1, 2, 3, 4)]
    peers += [at_x(k) for k in range(1, 4)] + [at_z(k) for k in range(1, 8)]
    sent = []

    class Send:
        def __init__(self, src, dst, device, leaves=None, comes=None):
            i = len(sent)
            self.copy = pltpu.make_async_remote_copy(
                src_ref=src, dst_ref=dst, send_sem=ssem.at[i], recv_sem=rsem.at[i],
                device_id=device, device_id_type=MESH,
            )
            self.leaves, self.comes = leaves, comes
            self.act(leaves, self.copy.start)
            sent.append(self)

        def act(self, condition, action):
            if condition is None:
                action()
            else:
                pl.when(condition)(action)

        def wait_recv(self):
            self.act(self.comes, self.copy.wait_recv)

        def wait_send(self):
            self.act(self.leaves, self.copy.wait_send)

    def near_slab(src, dst, distance):
        return Send(src, dst, at_slab(distance), inside(distance), inside(-distance))

    def rows(count, index):
        return pl.ds(pl.multiple_of(count * index, count), count)

    barrier = pltpu.get_barrier_semaphore()
    for peer in peers:
        pl.semaphore_signal(barrier, inc=1, device_id=peer, device_id_type=MESH)
    loads = [
        pltpu.make_async_copy(src, dst, lsem.at[i])
        for i, (src, dst) in enumerate((
            (q_hbm, q_ref), (head_hbm, head.at[rows(256, m)]), (p_hbm, p_ref),
            (mask_hbm, mask_ref), (pos_hbm, pos_ref), (weight_hbm, weight_ref),
        ))
    ]
    for copy in loads:
        copy.start()

    for k in (-4, -3, -2, -1, 1, 2, 3, 4):
        @pl.when(jnp.logical_not(inside(k)))
        def _():
            ttr[k + 4] = jnp.zeros((4, 128), F32)
            if abs(k) <= 2:
                qb[(2 + k) * QM : (3 + k) * QM] = jnp.zeros((QM, D), BF)
                gr[k + 2] = jnp.zeros((QM, D), BF)
                auxr[k + 2] = jnp.zeros((8, 128), F32)

    loads[0].wait()
    loads[1].wait()
    own_head = head[rows(256, m)]
    part_q[...] = jnp.dot(q_ref[...], own_head, preferred_element_type=F32).astype(BF)
    pl.semaphore_wait(barrier, len(peers))
    q1 = Send(part_q.at[rows(QM, osib)], rq.at[1], to_sib)
    q0 = Send(part_q.at[rows(QM, sib)], rq.at[0], to_sib)
    mine = head.at[rows(256, m)]
    heads = [Send(mine, mine, to_back)]
    loads[2].wait()
    part_p[...] = jnp.dot(p_ref[...], own_head, preferred_element_type=F32).astype(BF)
    p1 = Send(part_p.at[rows(PM, osib)], rp.at[1], to_sib)
    p0 = Send(part_p.at[rows(PM, sib)], rp.at[0], to_sib)
    q1.wait_recv()
    yq[...] = (part_q[rows(QM, opp)].astype(F32) + rq[1].astype(F32)).astype(BF)
    q2 = Send(yq, zq, to_opp)
    p1.wait_recv()
    yp[...] = (part_p[rows(PM, opp)].astype(F32) + rp[1].astype(F32)).astype(BF)
    p2 = Send(yp, zp, to_opp)

    def own_lanes(value):
        quarters = [value[:, k * QM : (k + 1) * QM] for k in range(4)]
        return jnp.where(
            m == 0, quarters[0],
            jnp.where(m == 1, quarters[1], jnp.where(m == 2, quarters[2], quarters[3])),
        )

    for copy in loads[3:]:
        copy.wait()
    count = counts_ref[slab]
    count_f = count.astype(F32)
    weight = own_lanes(weight_ref[...])
    slot = own_lanes(pos_ref[...].astype(F32))
    wanted = slot - count_f * jnp.floor((slot + 0.5) / count_f)
    auxs[...] = jnp.zeros_like(auxs)
    for k in range(5):
        auxs[k, 0:4, 0:QM] = own_lanes(mask_ref[k].astype(F32))
        auxs[k, 4:5, 0:QM] = weight
    xo[0:QM, rows(256, m)] = q_ref[rows(QM, m)]
    xo[QM:, rows(256, m)] = p_ref[rows(PM, m)]

    def normalise(projected):
        norm = jnp.sqrt(jnp.sum(projected * projected, axis=1, keepdims=True) + EPS)
        return projected / norm, norm

    q0.wait_recv()
    q2.wait_recv()
    unit, norm = normalise(
        part_q[rows(QM, m)].astype(F32) + rq[0].astype(F32) + zq[...].astype(F32)
    )
    unit_q[...] = unit
    norm_q[...] = norm
    qb[2 * QM : 3 * QM] = unit.astype(BF)
    queries, auxes = [], []
    for k in (1, -1, 2, -2):
        queries.append(
            near_slab(qb.at[2 * QM : 3 * QM], qb.at[(2 - k) * QM : (3 - k) * QM], k)
        )
        auxes.append(near_slab(auxs.at[2 + k], auxr.at[2 - k], k))

    p0.wait_recv()
    p2.wait_recv()
    unit, norm = normalise(
        part_p[rows(PM, m)].astype(F32) + rp[0].astype(F32) + zp[...].astype(F32)
    )
    unit_p[...] = unit
    norm_p[...] = norm
    pb[rows(PM, m)] = unit.astype(BF)

    def piece(member, part):
        return pb.at[pl.ds(pl.multiple_of(member * PM + part * 64, 64), 64)]

    over = [Send(piece(m, h), piece(m, h), to_opp) for h in range(2)]
    near = Send(pb.at[rows(PM, m)], pb.at[rows(PM, m)], to_sib)
    wide = []
    for member, device in ((opp, to_opp), (osib, to_osib), (sib, to_sib)):
        wide.append(
            Send(q_ref.at[rows(QM, member)], xo.at[0:QM, rows(256, m)], device)
        )
        wide.append(
            Send(p_ref.at[rows(PM, member)], xo.at[QM : QM + PM, rows(256, m)], device)
        )
    far = []
    for h in range(2):
        over[h].wait_recv()
        far.append(Send(piece(opp, h), piece(opp, h), to_sib))
    heads.append(Send(mine, mine, to_sib))
    for copy in [near] + far:
        copy.wait_recv()
    for copy in queries + auxes:
        copy.wait_recv()

    auxr[2] = auxs[2]
    for k in range(5):
        lanes = slice(k * QM, (k + 1) * QM)
        auxc[:, lanes] = auxr[k][:, 0:QM]
        auxc[5:6, lanes] = wanted if k == 2 else jnp.full((1, QM), -1.0, F32)
    scores = lax.dot_general(
        pb[...], qb[...], (((1,), (1,)), ((), ())), preferred_element_type=F32
    )
    slot_ids = lax.broadcasted_iota(jnp.int32, (PM, NQ), 0)
    others = jnp.zeros((1, NQ), F32)
    positive = jnp.zeros((1, NQ), F32)
    for tile in range(4):
        ids = slot_ids + tile * PM
        is_positive = ids.astype(F32) == auxc[5:6, :]
        kept = (ids < count) & (auxc[tile : tile + 1, :] > 0.5) & jnp.logical_not(is_positive)
        grown = jnp.exp(scores[tile * PM : (tile + 1) * PM] / TAU)
        terms = jnp.where(kept, grown, 0.0)
        others = others + jnp.sum(terms, axis=0, keepdims=True)
        positive = positive + jnp.sum(jnp.where(is_positive, grown, 0.0), axis=0, keepdims=True)
        ef[tile * PM : (tile + 1) * PM] = terms
        eb[tile * PM : (tile + 1) * PM] = terms.astype(BF)
    for k in range(5):
        tts[k // 2 : k // 2 + 1, (k % 2) * QM : (k % 2 + 1) * QM] = others[
            :, k * QM : (k + 1) * QM
        ]
    tts[2:3, QM:128] = positive[:, 2 * QM : 3 * QM]
    tts[3:4, :] = jnp.zeros((1, 128), F32)
    totals = [near_slab(tts, ttr.at[4 - k], k) for k in (1, -1, 2, -2, 3, -3, 4, -4)]

    terms = lax.dot_general(
        eb[...], pb[...], (((0,), (0,)), ((), ())), preferred_element_type=F32
    )
    returns = []
    for k in (2, -2, 1, -1):
        gs[2 + k] = terms[(2 + k) * QM : (3 + k) * QM].astype(BF)
        returns.append(near_slab(gs.at[2 + k], gr.at[2 - k], k))
    own_terms = terms[2 * QM : 3 * QM]

    ttr[4] = tts[...]
    heads[0].wait_recv()
    theirs = head.at[rows(256, opp)]
    heads.append(Send(theirs, theirs, to_sib))
    for copy in totals:
        copy.wait_recv()
    for k in range(-2, 3):
        rest = jnp.zeros((1, QM), F32)
        for j in range(-2, 3):
            n = 2 - j
            rest = rest + ttr[k + j + 4][n // 2 : n // 2 + 1, (n % 2) * QM : (n % 2 + 1) * QM]
        whole = rest + ttr[k + 4][2:3, QM:128]
        lanes = slice((2 + k) * QM, (3 + k) * QM)
        scale = auxc[4:5, lanes] / (whole * TAU)
        auxc[6:7, lanes] = jnp.where(inside(k), scale, 0.0)
        if k == 0:
            own_rest, own_whole = rest, whole
            auxc[7:8, lanes] = scale * rest
        else:
            auxc[7:8, lanes] = jnp.zeros((1, QM), F32)

    for tile in range(4):
        here = slice(tile * PM, (tile + 1) * PM)
        is_positive = (slot_ids + tile * PM).astype(F32) == auxc[5:6, :]
        coefficient = jnp.where(is_positive, -auxc[7:8, :], ef[here] * auxc[6:7, :])
        part = jnp.dot(coefficient.astype(BF), qb[...], preferred_element_type=F32)
        ppf[here] = part
        pps[here] = part.astype(BF)
    p1 = Send(pps.at[rows(PM, osib)], pr.at[1], to_sib)
    p0 = Send(pps.at[rows(PM, sib)], pr.at[0], to_sib)
    p1.wait_recv()
    py[...] = (ppf[rows(PM, opp)] + pr[1].astype(F32)).astype(BF)
    p2 = Send(py, pz, to_opp)

    def tangent(unit, norm, grad):
        radial = jnp.sum(unit * grad, axis=1, keepdims=True)
        return ((grad - unit * radial) / norm).astype(BF)

    eye = lax.broadcasted_iota(jnp.int32, (QM, QM), 0) == lax.broadcasted_iota(
        jnp.int32, (QM, QM), 1
    )

    def column(row):
        return jnp.sum(jnp.where(eye, row, 0.0), axis=1, keepdims=True)

    one_hot = (
        lax.broadcasted_iota(jnp.int32, (4 * PM, QM), 0).astype(F32) == wanted
    ).astype(F32).astype(BF)
    chosen = lax.dot_general(
        one_hot, pb[...], (((0,), (0,)), ((), ())), preferred_element_type=F32
    )
    scale = column(weight / (own_whole * TAU))
    drop = column(weight * own_rest / (own_whole * TAU))
    for copy in returns:
        copy.wait_recv()
    for k in (0, 1, 3, 4):
        own_terms = own_terms + gr[k].astype(F32)
    pgo[0:QM] = tangent(unit_q[...], norm_q[...], own_terms * scale - chosen * drop)
    p0.wait_recv()
    p2.wait_recv()
    summed = ppf[rows(PM, m)] + pr[0].astype(F32) + pz[...].astype(F32)
    pgo[QM:] = tangent(unit_p[...], norm_p[...], summed)

    for copy in wide:
        copy.wait_recv()

    def cols(size, index):
        return pl.ds(pl.multiple_of(index * size, size), size)

    def term(block, half, owner):
        features = cols(128, (2 * block + owner) * 2 + half)
        return lax.dot_general(
            xo[:, features], pgo[...], (((0,), (0,)), ((), ())), preferred_element_type=F32
        )

    pairs = []
    for half in range(2):
        for block in range(2):
            there = slice(half * 128, (half + 1) * 128)
            tsend[block, there] = term(block, half, 1 - core).astype(BF)
            pairs.append(Send(tsend.at[block, there], trecv.at[block, there], to_sib))
    for half in range(2):
        for block in range(2):
            there = slice(half * 128, (half + 1) * 128)
            hf[block, there] = term(block, half, core)

    first = []
    for half in range(2):
        there = slice(half * 128, (half + 1) * 128)
        for block in range(2):
            pairs[2 * half + block].wait_recv()
            total = hf[block, there] + trecv[block, there].astype(F32)
            hf[block, there] = total
            hb[block, there] = total.astype(BF)
        if half == 0:
            for k in (2, 1, 3):
                first.append(
                    Send(hb.at[:, there, cols(256, (xi + k) % 4)], ax.at[k - 1], at_x(k))
                )
        else:
            first.append(Send(hb.at[low, there, cols(512, 1 - high)], cy.at[2], to_high))
            first.append(Send(hb.at[1 - low, there, cols(512, high)], cy.at[0], to_opp))
            first.append(Send(hb.at[1 - low, there, cols(512, 1 - high)], cy.at[1], to_back))

    for copy in heads[1:]:
        copy.wait_recv()
    eo[...] = lax.dot_general(
        pgo[...], head[...], (((1,), (1,)), ((), ())), preferred_element_type=F32
    ).astype(BF)
    oq_ref[rows(QM, m)] = eo[0:QM, cols(256, m)]
    op_ref[rows(PM, m)] = eo[QM:, cols(256, m)]

    def spread(member, device):
        return [
            Send(eo.at[0:QM, cols(256, member)], oq_ref.at[rows(QM, m)], device),
            Send(eo.at[QM : QM + PM, cols(256, member)], op_ref.at[rows(PM, m)], device),
        ]

    outs = spread(sib, to_sib)

    for copy in first[:3]:
        copy.wait_recv()
    total = hf[:, 0:128, cols(256, xi)]
    for k in range(3):
        total = total + ax[k].astype(F32)
    a1f[...] = total
    a1[...] = total.astype(BF)
    second = [
        Send(a1.at[low, :, cols(128, 1 - high)], ay.at[2], to_high),
        Send(a1.at[1 - low, :, cols(128, high)], ay.at[0], to_opp),
        Send(a1.at[1 - low, :, cols(128, 1 - high)], ay.at[1], to_back),
    ]
    for copy in first[3:]:
        copy.wait_recv()
    total = hf[low, 128:256, cols(512, high)]
    for k in range(3):
        total = total + cy[k].astype(F32)
    c1f[...] = total
    c1[...] = total.astype(BF)
    for k in (2, 1, 3):
        second.append(Send(c1.at[:, cols(128, (xi + k) % 4)], cx.at[k - 1], at_x(k)))
    for copy in second:
        copy.wait_recv()
    total = a1f[low, :, cols(128, high)]
    for k in range(3):
        total = total + ay[k].astype(F32)
    e1f[0:128] = total
    e1[0:128] = total.astype(BF)
    total = c1f[:, cols(128, xi)]
    for k in range(3):
        total = total + cx[k].astype(F32)
    e1f[128:256] = total
    e1[128:256] = total.astype(BF)
    third = []
    for k in (4, 3, 5, 2, 6, 1, 7):
        third.append(Send(e1.at[rows(32, (zi + k) % 8)], ez.at[k - 1], at_z(k)))
    outs += spread(opp, to_opp) + spread(osib, to_osib)
    for copy in third:
        copy.wait_recv()
    total = e1f[rows(32, zi)]
    for k in range(7):
        total = total + ez[k].astype(F32)
    gz[rows(32, zi)] = total.astype(BF)
    fourth = []
    for k in (4, 3, 5, 2, 6, 1, 7):
        fourth.append(Send(gz.at[rows(32, zi)], gz.at[rows(32, zi)], at_z(k)))
    for copy in fourth:
        copy.wait_recv()
    upper = cols(128, 2 * xi + high)
    lower = cols(128, 4 * high + xi)
    oh_ref[0:128, upper] = gz[0:128]
    oh_ref[128:256, lower] = gz[128:256]
    mine = oh_ref.at[0:128, upper]
    fifth = [Send(mine, mine, to_high)]
    mine = oh_ref.at[128:256, lower]
    for k in (2, 1, 3):
        fifth.append(Send(mine, mine, at_x(k)))
    fifth[0].wait_recv()
    last = []
    mine = oh_ref.at[0:128, cols(256, xi)]
    for k in (2, 1, 3):
        last.append(Send(mine, mine, at_x(k)))
    for copy in fifth[1:]:
        copy.wait_recv()
    mine = oh_ref.at[128:256, cols(512, high)]
    last.append(Send(mine, mine, to_high))
    for copy in outs + last:
        copy.wait_recv()
    for copy in sent:
        copy.wait_send()


def body(query_emb, passage_emb, head, fn_mask, counts, positive_slot, query_weight):
    vmem = pl.BlockSpec(memory_space=pltpu.VMEM)
    hbm = pl.BlockSpec(memory_space=pl.ANY)
    smem = pl.BlockSpec(memory_space=pltpu.SMEM)

    def half(*shape):
        return pltpu.VMEM(shape, BF)

    def full(*shape):
        return pltpu.VMEM(shape, F32)

    query_grad, passage_grad, head_grad = pl.pallas_call(
        kernel,
        out_shape=(
            jax.ShapeDtypeStruct((256, 256), BF),
            jax.ShapeDtypeStruct((512, 256), BF),
            jax.ShapeDtypeStruct((256, D), BF),
        ),
        in_specs=[hbm, hbm, hbm, hbm, smem, hbm, hbm],
        out_specs=(vmem, vmem, vmem),
        scratch_shapes=[
            half(256, 256), half(512, 256), half(D, D),
            pltpu.VMEM((5, 4, 256), jnp.int32), pltpu.VMEM((1, 256), jnp.int32), full(1, 256),
            half(256, D), half(512, D), half(2, QM, D), half(2, PM, D),
            half(QM, D), half(PM, D), half(QM, D), half(PM, D),
            full(QM, D), full(PM, D), full(QM, 1), full(PM, 1),
            half(NQ, D), half(4 * PM, D), full(5, 8, 128), full(5, 8, 128), full(8, NQ),
            full(4 * PM, NQ), half(4 * PM, NQ), full(4, 128), full(9, 4, 128),
            half(5, QM, D), half(5, QM, D),
            half(512, D), full(512, D), half(2, PM, D), half(PM, D), half(PM, D),
            half(QM + PM, D), half(QM + PM, D), half(QM + PM, D),
            half(2, 256, D), half(2, 256, D), full(2, 256, D), half(2, 256, D),
            half(3, 2, 128, 256), half(3, 128, 512),
            full(2, 128, 256), full(128, 512), half(2, 128, 256), half(128, 512),
            half(3, 128, 128), half(3, 128, 128), full(256, 128), half(256, 128),
            half(7, 32, 128), half(256, 128),
            pltpu.SemaphoreType.DMA((6,)),
            pltpu.SemaphoreType.DMA((SEMS,)), pltpu.SemaphoreType.DMA((SEMS,)),
        ],
        compiler_params=pltpu.CompilerParams(
            collective_id=0, has_side_effects=True, vmem_limit_bytes=48 << 20
        ),
        cost_estimate=pl.CostEstimate(flops=3 << 30, bytes_accessed=4 << 20, transcendentals=0),
    )(
        query_emb, passage_emb, head, jnp.transpose(fn_mask, (1, 2, 0)), counts,
        positive_slot.reshape(1, -1), query_weight.reshape(1, -1),
    )
    return query_grad, passage_grad, head_grad.astype(F32)


def solution(mesh):
    return jax.shard_map(
        body,
        mesh=mesh,
        in_specs=(
            P("slab", "mp"), P("slab", "mp"), P("mp", None), P("slab", None, None),
            P(), P("slab"), P("slab"),
        ),
        out_specs=(P("slab", "mp"), P("slab", "mp"), P("mp", None)),
        check_vma=False,
    )
```

```python
import jax
import jax.numpy as jnp
from jax import lax
from jax.experimental import pallas as pl
from jax.experimental.pallas import tpu as pltpu
from jax.sharding import PartitionSpec as P

EPS = 1e-06
TAU = 0.05
D = 1024
QM = 64
PM = 128
NQ = 5 * QM
SEMS = 112
MESH = pl.DeviceIdType.MESH
BF = jnp.bfloat16
F32 = jnp.float32


def kernel(
    q_hbm, p_hbm, head_hbm, mask_hbm, counts_hbm, pos_hbm, weight_hbm,
    oq_ref, op_ref, oh_ref,
    q_ref, p_ref, head, mask_ref, counts_ref, pos_ref, weight_ref,
    part_q, rq, yq, zq, xh, unit_q, unit_p, norm_q, norm_p,
    qb, pb, auxs, auxr, auxc, ef, eb, tts, ttr, gs, gr,
    pps, pr, py, pz, xo, pgt, eo,
    hf, hb, ax, cy, a1f, c1f, a1, c1, ay, cx, e1f, e1, ez, gz,
    lsem, ssem, rsem,
):
    slab = lax.axis_index("slab")
    m = lax.axis_index("mp")
    core, low = m % 2, m // 2
    sib = 2 * low + 1 - core
    opp = 2 * (1 - low) + core
    osib = 2 * (1 - low) + 1 - core
    high, xi, zi = slab // 32, (slab // 8) % 4, slab % 8
    p_own, p_sib = 2 * core + low, 2 * (1 - core) + low
    p_opp, p_osib = 2 * core + 1 - low, 2 * (1 - core) + 1 - low

    def at_slab(distance):
        there = (slab + distance + 64) % 64
        return (there, jnp.where(there // 32 == high, m, opp))

    def at_x(step):
        return (high * 32 + ((xi + step) % 4) * 8 + zi, m)

    def at_z(step):
        return (high * 32 + xi * 8 + (zi + step) % 8, m)

    def inside(distance):
        return jnp.logical_and(slab + distance >= 0, slab + distance < 64)

    to_sib, to_opp, to_osib = (slab, sib), (slab, opp), (slab, osib)
    to_high, to_back = ((slab + 32) % 64, m), ((slab + 32) % 64, opp)
    peers = [to_sib, to_opp, to_osib, to_high, to_back]
    peers += [at_slab(k) for k in (-4, -3, -2, -1, 1, 2, 3, 4)]
    peers += [at_x(k) for k in range(1, 4)] + [at_z(k) for k in range(1, 8)]
    sent = []

    class Send:
        def __init__(self, src, dst, device, leaves=None, comes=None):
            i = len(sent)
            self.copy = pltpu.make_async_remote_copy(
                src_ref=src, dst_ref=dst, send_sem=ssem.at[i], recv_sem=rsem.at[i],
                device_id=device, device_id_type=MESH,
            )
            self.leaves, self.comes = leaves, comes
            self.act(leaves, self.copy.start)
            sent.append(self)

        def act(self, condition, action):
            if condition is None:
                action()
            else:
                pl.when(condition)(action)

        def wait_recv(self):
            self.act(self.comes, self.copy.wait_recv)

        def wait_send(self):
            self.act(self.leaves, self.copy.wait_send)

    def near_slab(src, dst, distance):
        return Send(src, dst, at_slab(distance), inside(distance), inside(-distance))

    def rows(count, index):
        return pl.ds(pl.multiple_of(count * index, count), count)

    barrier = pltpu.get_barrier_semaphore()
    for peer in peers:
        pl.semaphore_signal(barrier, inc=1, device_id=peer, device_id_type=MESH)
    loads = [
        pltpu.make_async_copy(src, dst, lsem.at[i])
        for i, (src, dst) in enumerate((
            (q_hbm, q_ref), (head_hbm, head.at[rows(256, m)]), (p_hbm, p_ref),
            (mask_hbm, mask_ref), (counts_hbm, counts_ref), (pos_hbm, pos_ref),
            (weight_hbm, weight_ref),
        ))
    ]
    for copy in loads:
        copy.start()

    for k in (-4, -3, -2, -1, 1, 2, 3, 4):
        @pl.when(jnp.logical_not(inside(k)))
        def _():
            ttr[k + 4] = jnp.zeros((4, 128), F32)
            if abs(k) <= 2:
                qb[(2 + k) * QM : (3 + k) * QM] = jnp.zeros((QM, D), BF)
                gr[k + 2] = jnp.zeros((QM, D), BF)
                auxr[k + 2] = jnp.zeros((8, 128), F32)

    loads[0].wait()
    loads[1].wait()
    own_head = head[rows(256, m)]
    part_q[...] = jnp.dot(q_ref[...], own_head, preferred_element_type=F32).astype(BF)
    pl.semaphore_wait(barrier, len(peers))
    q1 = Send(part_q.at[rows(QM, osib)], rq.at[1], to_sib)
    q0 = Send(part_q.at[rows(QM, sib)], rq.at[0], to_sib)

    def head_rows(member, start, size):
        return head.at[pl.ds(pl.multiple_of(member * 256 + start, 16), size)]

    heads = []
    for start, size in ((0, 112), (112, 112)):
        mine = head_rows(m, start, size)
        heads.append(Send(mine, mine, to_back))
    near_head = Send(head_rows(m, 0, 256), head_rows(m, 0, 256), to_sib)
    q1.wait_recv()
    yq[...] = (part_q[rows(QM, opp)].astype(F32) + rq[1].astype(F32)).astype(BF)
    q2 = Send(yq, zq, to_opp)

    loads[2].wait()
    feature = rows(256, m)
    wide = [
        Send(p_ref.at[rows(256, core)], xh.at[:, feature], to_opp),
        Send(p_ref.at[rows(256, 1 - core)], xh.at[:, feature], to_osib),
        Send(p_ref.at[rows(256, 1 - core)], xh.at[:, feature], to_sib),
    ]
    xh[:, feature] = p_ref[rows(256, core)]
    mine = head_rows(m, 224, 32)
    heads.append(Send(mine, mine, to_opp))

    def own_lanes(value):
        quarters = [value[:, k * QM : (k + 1) * QM] for k in range(4)]
        return jnp.where(
            m == 0, quarters[0],
            jnp.where(m == 1, quarters[1], jnp.where(m == 2, quarters[2], quarters[3])),
        )

    for copy in loads[3:]:
        copy.wait()
    count = counts_ref[slab]
    count_f = count.astype(F32)
    weight = own_lanes(weight_ref[...])
    slot = own_lanes(pos_ref[...].astype(F32))
    wanted = slot - count_f * jnp.floor((slot + 0.5) / count_f)
    auxs[...] = jnp.zeros_like(auxs)
    for k in range(5):
        auxs[k, 0:4, 0:QM] = own_lanes(mask_ref[k].astype(F32))
        auxs[k, 4:5, 0:QM] = weight
    xo[0:QM, rows(256, low)] = q_ref[rows(QM, m)]
    xo[QM:192, rows(256, low)] = p_ref[rows(PM, p_own)]
    xo[192 : 192 + QM, rows(256, low)] = q_ref[rows(QM, sib)]
    xo[192 + QM :, rows(256, low)] = p_ref[rows(PM, p_sib)]

    def normalise(projected):
        norm = jnp.sqrt(jnp.sum(projected * projected, axis=1, keepdims=True) + EPS)
        return projected / norm, norm

    q0.wait_recv()
    q2.wait_recv()
    unit, norm = normalise(
        part_q[rows(QM, m)].astype(F32) + rq[0].astype(F32) + zq[...].astype(F32)
    )
    unit_q[...] = unit
    norm_q[...] = norm
    qb[2 * QM : 3 * QM] = unit.astype(BF)
    queries, auxes = [], []
    for k in (1, -1, 2, -2):
        queries.append(
            near_slab(qb.at[2 * QM : 3 * QM], qb.at[(2 - k) * QM : (3 - k) * QM], k)
        )
        auxes.append(near_slab(auxs.at[2 + k], auxr.at[2 - k], k))

    wide_q = [
        Send(q_ref.at[rows(QM, member)], xo.at[first : first + QM, rows(256, low)], to_opp)
        for first, member in ((0, opp), (192, osib))
    ]

    def chip_part(chip):
        features = rows(512, chip)
        return jnp.dot(xh[:, features], head[features], preferred_element_type=F32)

    wide[2].wait_recv()
    near_head.wait_recv()
    projected = chip_part(low)
    far_heads = []
    for copy, (start, size) in ((heads[0], (0, 112)), (heads[2], (224, 32)), (heads[1], (112, 112))):
        copy.wait_recv()
        theirs = head_rows(opp, start, size)
        far_heads.append(Send(theirs, theirs, to_sib))
    for copy in wide[:2] + far_heads:
        copy.wait_recv()
    unit, norm = normalise(projected + chip_part(1 - low))
    unit_p[...] = unit
    norm_p[...] = norm
    pb[rows(256, core)] = unit.astype(BF)
    mine = pb.at[rows(256, core)]
    near = Send(mine, mine, to_sib)
    xo[QM:192, rows(256, 1 - low)] = xh[rows(PM, low), rows(256, opp)]
    wide_q.append(
        Send(xh.at[rows(PM, low), rows(256, osib)], xo.at[192 + QM : 384, rows(256, 1 - low)], to_sib)
    )
    near.wait_recv()
    for copy in queries + auxes:
        copy.wait_recv()

    auxr[2] = auxs[2]
    for k in range(5):
        lanes = slice(k * QM, (k + 1) * QM)
        auxc[:, lanes] = auxr[k][:, 0:QM]
        auxc[5:6, lanes] = wanted if k == 2 else jnp.full((1, QM), -1.0, F32)
    scores = lax.dot_general(
        pb[...], qb[...], (((1,), (1,)), ((), ())), preferred_element_type=F32
    )
    slot_ids = lax.broadcasted_iota(jnp.int32, (PM, NQ), 0)
    others = jnp.zeros((1, NQ), F32)
    positive = jnp.zeros((1, NQ), F32)
    for tile in range(4):
        ids = slot_ids + tile * PM
        is_positive = ids.astype(F32) == auxc[5:6, :]
        kept = (ids < count) & (auxc[tile : tile + 1, :] > 0.5) & jnp.logical_not(is_positive)
        grown = jnp.exp(scores[tile * PM : (tile + 1) * PM] / TAU)
        terms = jnp.where(kept, grown, 0.0)
        others = others + jnp.sum(terms, axis=0, keepdims=True)
        positive = positive + jnp.sum(jnp.where(is_positive, grown, 0.0), axis=0, keepdims=True)
        ef[tile * PM : (tile + 1) * PM] = terms
        eb[tile * PM : (tile + 1) * PM] = terms.astype(BF)
    for k in range(5):
        tts[k // 2 : k // 2 + 1, (k % 2) * QM : (k % 2 + 1) * QM] = others[
            :, k * QM : (k + 1) * QM
        ]
    tts[2:3, QM:128] = positive[:, 2 * QM : 3 * QM]
    tts[3:4, :] = jnp.zeros((1, 128), F32)
    totals = [near_slab(tts, ttr.at[4 - k], k) for k in (1, -1, 2, -2, 3, -3, 4, -4)]

    terms = lax.dot_general(
        eb[...], pb[...], (((0,), (0,)), ((), ())), preferred_element_type=F32
    )
    returns = []
    for k in (2, -2, 1, -1):
        gs[2 + k] = terms[(2 + k) * QM : (3 + k) * QM].astype(BF)
        returns.append(near_slab(gs.at[2 + k], gr.at[2 - k], k))
    own_terms = terms[2 * QM : 3 * QM]

    ttr[4] = tts[...]
    for copy in totals:
        copy.wait_recv()
    for k in range(-2, 3):
        rest = jnp.zeros((1, QM), F32)
        for j in range(-2, 3):
            n = 2 - j
            rest = rest + ttr[k + j + 4][n // 2 : n // 2 + 1, (n % 2) * QM : (n % 2 + 1) * QM]
        whole = rest + ttr[k + 4][2:3, QM:128]
        lanes = slice((2 + k) * QM, (3 + k) * QM)
        scale = auxc[4:5, lanes] / (whole * TAU)
        auxc[6:7, lanes] = jnp.where(inside(k), scale, 0.0)
        if k == 0:
            own_rest, own_whole = rest, whole
            auxc[7:8, lanes] = scale * rest
        else:
            auxc[7:8, lanes] = jnp.zeros((1, QM), F32)

    def passage_terms(index):
        is_positive = (slot_ids + index * PM).astype(F32) == auxc[5:6, :]
        coefficient = jnp.where(is_positive, -auxc[7:8, :], ef[rows(PM, index)] * auxc[6:7, :])
        return jnp.dot(coefficient.astype(BF), qb[...], preferred_element_type=F32)

    pps[1] = passage_terms(p_osib).astype(BF)
    pieces = [slice(0, 64), slice(64, 128)]
    p1 = [Send(pps.at[1, piece], pr.at[1, piece], to_sib) for piece in pieces]
    part = passage_terms(p_opp)
    p2 = []
    for copy, piece in zip(p1, pieces):
        copy.wait_recv()
        py[piece] = (part[piece] + pr[1, piece].astype(F32)).astype(BF)
        p2.append(Send(py.at[piece], pz.at[piece], to_opp))
    pps[0] = passage_terms(p_sib).astype(BF)
    p0 = Send(pps.at[0], pr.at[0], to_sib)
    own_part = passage_terms(p_own)

    def tangent(unit, norm, grad):
        radial = jnp.sum(unit * grad, axis=1, keepdims=True)
        return ((grad - unit * radial) / norm).astype(BF)

    eye = lax.broadcasted_iota(jnp.int32, (QM, QM), 0) == lax.broadcasted_iota(
        jnp.int32, (QM, QM), 1
    )

    def column(row):
        return jnp.sum(jnp.where(eye, row, 0.0), axis=1, keepdims=True)

    one_hot = (
        lax.broadcasted_iota(jnp.int32, (4 * PM, QM), 0).astype(F32) == wanted
    ).astype(F32).astype(BF)
    chosen = lax.dot_general(
        one_hot, pb[...], (((0,), (0,)), ((), ())), preferred_element_type=F32
    )
    scale = column(weight / (own_whole * TAU))
    drop = column(weight * own_rest / (own_whole * TAU))
    for copy in returns:
        copy.wait_recv()
    for k in (0, 1, 3, 4):
        own_terms = own_terms + gr[k].astype(F32)
    pgt[0:QM] = tangent(unit_q[...], norm_q[...], own_terms * scale - chosen * drop)
    shared = [Send(pgt.at[0:QM], pgt.at[192 : 192 + QM], to_sib)]
    for copy in [p0] + p2:
        copy.wait_recv()
    summed = own_part + pr[0].astype(F32) + pz[...].astype(F32)
    pgt[QM:192] = tangent(unit_p[rows(PM, low)], norm_p[rows(PM, low)], summed)
    shared.append(Send(pgt.at[QM:192], pgt.at[192 + QM : 384], to_sib))

    def cols(size, index):
        return pl.ds(pl.multiple_of(index * size, size), size)

    for copy in wide_q + shared:
        copy.wait_recv()

    first = []
    for half in range(2):
        there = slice(half * 128, (half + 1) * 128)
        for block in range(2):
            features = slice(block * 256 + half * 128, block * 256 + (half + 1) * 128)
            total = lax.dot_general(
                xo[:, features], pgt[...], (((0,), (0,)), ((), ())), preferred_element_type=F32
            )
            hf[block, there] = total
            hb[block, there] = total.astype(BF)
        if half == 0:
            for k in (2, 1, 3):
                first.append(
                    Send(hb.at[:, there, cols(256, (xi + k) % 4)], ax.at[k - 1], at_x(k))
                )
        else:
            first.append(Send(hb.at[low, there, cols(512, 1 - high)], cy.at[2], to_high))
            first.append(Send(hb.at[1 - low, there, cols(512, high)], cy.at[0], to_opp))
            first.append(Send(hb.at[1 - low, there, cols(512, 1 - high)], cy.at[1], to_back))

    eo[...] = lax.dot_general(
        pgt[0:192], head[...], (((1,), (1,)), ((), ())), preferred_element_type=F32
    ).astype(BF)
    oq_ref[rows(QM, m)] = eo[0:QM, cols(256, m)]
    op_ref[rows(PM, p_own)] = eo[QM:, cols(256, m)]

    def spread(member, device):
        return [
            Send(eo.at[0:QM, cols(256, member)], oq_ref.at[rows(QM, m)], device),
            Send(eo.at[QM : QM + PM, cols(256, member)], op_ref.at[rows(PM, p_own)], device),
        ]

    outs = spread(sib, to_sib)

    for copy in first[:3]:
        copy.wait_recv()
    total = hf[:, 0:128, cols(256, xi)]
    for k in range(3):
        total = total + ax[k].astype(F32)
    a1f[...] = total
    a1[...] = total.astype(BF)
    second = [
        Send(a1.at[low, :, cols(128, 1 - high)], ay.at[2], to_high),
        Send(a1.at[1 - low, :, cols(128, high)], ay.at[0], to_opp),
        Send(a1.at[1 - low, :, cols(128, 1 - high)], ay.at[1], to_back),
    ]
    for copy in first[3:]:
        copy.wait_recv()
    total = hf[low, 128:256, cols(512, high)]
    for k in range(3):
        total = total + cy[k].astype(F32)
    c1f[...] = total
    c1[...] = total.astype(BF)
    for k in (2, 1, 3):
        second.append(Send(c1.at[:, cols(128, (xi + k) % 4)], cx.at[k - 1], at_x(k)))
    for copy in second:
        copy.wait_recv()
    total = a1f[low, :, cols(128, high)]
    for k in range(3):
        total = total + ay[k].astype(F32)
    e1f[0:128] = total
    e1[0:128] = total.astype(BF)
    total = c1f[:, cols(128, xi)]
    for k in range(3):
        total = total + cx[k].astype(F32)
    e1f[128:256] = total
    e1[128:256] = total.astype(BF)
    third = []
    for k in (4, 3, 5, 2, 6, 1, 7):
        third.append(Send(e1.at[rows(32, (zi + k) % 8)], ez.at[k - 1], at_z(k)))
    outs += spread(opp, to_opp) + spread(osib, to_osib)
    for copy in third:
        copy.wait_recv()
    total = e1f[rows(32, zi)]
    for k in range(7):
        total = total + ez[k].astype(F32)
    gz[rows(32, zi)] = total.astype(BF)
    fourth = []
    for k in (4, 3, 5, 2, 6, 1, 7):
        fourth.append(Send(gz.at[rows(32, zi)], gz.at[rows(32, zi)], at_z(k)))
    for copy in fourth:
        copy.wait_recv()
    upper = cols(128, 2 * xi + high)
    lower = cols(128, 4 * high + xi)
    oh_ref[0:128, upper] = gz[0:128]
    oh_ref[128:256, lower] = gz[128:256]
    mine = oh_ref.at[0:128, upper]
    fifth = [Send(mine, mine, to_high)]
    mine = oh_ref.at[128:256, lower]
    for k in (2, 1, 3):
        fifth.append(Send(mine, mine, at_x(k)))
    fifth[0].wait_recv()
    last = []
    mine = oh_ref.at[0:128, cols(256, xi)]
    for k in (2, 1, 3):
        last.append(Send(mine, mine, at_x(k)))
    for copy in fifth[1:]:
        copy.wait_recv()
    mine = oh_ref.at[128:256, cols(512, high)]
    last.append(Send(mine, mine, to_high))
    for copy in outs + last:
        copy.wait_recv()
    for copy in sent:
        copy.wait_send()


def body(query_emb, passage_emb, head, fn_mask, counts, positive_slot, query_weight):
    vmem = pl.BlockSpec(memory_space=pltpu.VMEM)
    hbm = pl.BlockSpec(memory_space=pltpu.HBM)

    def half(*shape):
        return pltpu.VMEM(shape, BF)

    def full(*shape):
        return pltpu.VMEM(shape, F32)

    query_grad, passage_grad, head_grad = pl.pallas_call(
        kernel,
        out_shape=(
            jax.ShapeDtypeStruct((256, 256), BF),
            jax.ShapeDtypeStruct((512, 256), BF),
            jax.ShapeDtypeStruct((256, D), BF),
        ),
        in_specs=[hbm] * 7,
        out_specs=(vmem, vmem, vmem),
        scratch_shapes=[
            half(256, 256), half(512, 256), half(D, D),
            pltpu.VMEM((5, 4, 256), jnp.int32), pltpu.SMEM((64,), jnp.int32),
            pltpu.VMEM((1, 256), jnp.int32), full(1, 256),
            half(256, D), half(2, QM, D), half(QM, D), half(QM, D), half(256, D),
            full(QM, D), full(256, D), full(QM, 1), full(256, 1),
            half(NQ, D), half(4 * PM, D), full(5, 8, 128), full(5, 8, 128), full(8, NQ),
            full(4 * PM, NQ), half(4 * PM, NQ), full(4, 128), full(9, 4, 128),
            half(5, QM, D), half(5, QM, D),
            half(2, PM, D), half(2, PM, D), half(PM, D), half(PM, D),
            half(384, 512), half(384, D), half(192, D),
            full(2, 256, D), half(2, 256, D),
            half(3, 2, 128, 256), half(3, 128, 512),
            full(2, 128, 256), full(128, 512), half(2, 128, 256), half(128, 512),
            half(3, 128, 128), half(3, 128, 128), full(256, 128), half(256, 128),
            half(7, 32, 128), half(256, 128),
            pltpu.SemaphoreType.DMA((7,)),
            pltpu.SemaphoreType.DMA((SEMS,)), pltpu.SemaphoreType.DMA((SEMS,)),
        ],
        compiler_params=pltpu.CompilerParams(
            collective_id=0, has_side_effects=True, vmem_limit_bytes=48 << 20
        ),
        cost_estimate=pl.CostEstimate(flops=3 << 30, bytes_accessed=4 << 20, transcendentals=0),
    )(*[
        pltpu.with_memory_space_constraint(value, pltpu.HBM)
        for value in (
            query_emb, passage_emb, head, jnp.transpose(fn_mask, (1, 2, 0)), counts,
            positive_slot.reshape(1, -1), query_weight.reshape(1, -1),
        )
    ])
    return query_grad, passage_grad, head_grad.astype(F32)


def solution(mesh):
    return jax.shard_map(
        body,
        mesh=mesh,
        in_specs=(
            P("slab", "mp"), P("slab", "mp"), P("mp", None), P("slab", None, None),
            P(), P("slab"), P("slab"),
        ),
        out_specs=(P("slab", "mp"), P("slab", "mp"), P("mp", None)),
        check_vma=False,
    )
```

```python
import jax
import jax.numpy as jnp
from jax import lax
from jax.experimental import pallas as pl
from jax.experimental.pallas import tpu as pltpu
from jax.sharding import PartitionSpec as P

EPS = 1e-06
TAU = 0.05
D = 1024
QM = 64
PM = 128
NQ = 5 * QM
SEMS = 128
MESH = pl.DeviceIdType.MESH
BF = jnp.bfloat16
F32 = jnp.float32


def kernel(
    q_hbm, p_hbm, head_hbm, mask_hbm, counts_hbm, pos_hbm, weight_hbm,
    oq_ref, op_ref, oh_ref,
    q_ref, p_ref, head, mask_ref, counts_ref, pos_ref, weight_ref,
    part_q, rq, yq, zq, xh, unit_q, unit_p, norm_q, norm_p,
    qb, pb, auxs, auxr, auxc, ef, eb, tts, ttr, gs, gr,
    pps, pr, py, pz, xo, pgt, eo,
    hf, hb, ax, cy, a1f, c1f, a1, c1, ay, cx, e1f, e1, ez, gz, ga,
    lsem, ssem, rsem,
):
    slab = lax.axis_index("slab")
    m = lax.axis_index("mp")
    core, low = m % 2, m // 2
    sib = 2 * low + 1 - core
    opp = 2 * (1 - low) + core
    osib = 2 * (1 - low) + 1 - core
    high, xi, zi = slab // 32, (slab // 8) % 4, slab % 8
    p_own, p_sib = 2 * core + low, 2 * (1 - core) + low
    p_opp, p_osib = 2 * core + 1 - low, 2 * (1 - core) + 1 - low

    def at_slab(distance):
        there = (slab + distance + 64) % 64
        return (there, jnp.where(there // 32 == high, m, opp))

    def at_x(step):
        return (high * 32 + ((xi + step) % 4) * 8 + zi, m)

    def at_high_x(step):
        return ((1 - high) * 32 + ((xi + step) % 4) * 8 + zi, m)

    def at_z(step):
        return (high * 32 + xi * 8 + (zi + step) % 8, m)

    def inside(distance):
        return jnp.logical_and(slab + distance >= 0, slab + distance < 64)

    to_sib, to_opp, to_osib = (slab, sib), (slab, opp), (slab, osib)
    to_high, to_back = ((slab + 32) % 64, m), ((slab + 32) % 64, opp)
    peers = [to_sib, to_opp, to_osib, to_high, to_back]
    peers += [at_slab(k) for k in (-4, -3, -2, -1, 1, 2, 3, 4)]
    peers += [at_x(k) for k in range(1, 4)] + [at_z(k) for k in range(1, 8)]
    peers += [at_high_x(k) for k in range(1, 4)]
    sent = []

    class Send:
        def __init__(self, src, dst, device, leaves=None, comes=None):
            i = len(sent)
            self.copy = pltpu.make_async_remote_copy(
                src_ref=src, dst_ref=dst, send_sem=ssem.at[i], recv_sem=rsem.at[i],
                device_id=device, device_id_type=MESH,
            )
            self.leaves, self.comes = leaves, comes
            self.act(leaves, self.copy.start)
            sent.append(self)

        def act(self, condition, action):
            if condition is None:
                action()
            else:
                pl.when(condition)(action)

        def wait_recv(self):
            self.act(self.comes, self.copy.wait_recv)

        def wait_send(self):
            self.act(self.leaves, self.copy.wait_send)

    def near_slab(src, dst, distance):
        return Send(src, dst, at_slab(distance), inside(distance), inside(-distance))

    def rows(count, index):
        return pl.ds(pl.multiple_of(count * index, count), count)

    barrier = pltpu.get_barrier_semaphore()
    for peer in peers:
        pl.semaphore_signal(barrier, inc=1, device_id=peer, device_id_type=MESH)
    loads = [
        pltpu.make_async_copy(src, dst, lsem.at[i])
        for i, (src, dst) in enumerate((
            (q_hbm, q_ref), (head_hbm, head.at[rows(256, m)]), (p_hbm, p_ref),
            (mask_hbm, mask_ref), (counts_hbm, counts_ref), (pos_hbm, pos_ref),
            (weight_hbm, weight_ref),
        ))
    ]
    for copy in loads:
        copy.start()

    for k in (-4, -3, -2, -1, 1, 2, 3, 4):
        @pl.when(jnp.logical_not(inside(k)))
        def _():
            ttr[k + 4] = jnp.zeros((4, 128), F32)
            if abs(k) <= 2:
                qb[(2 + k) * QM : (3 + k) * QM] = jnp.zeros((QM, D), BF)
                gr[k + 2] = jnp.zeros((QM, D), BF)
                auxr[k + 2] = jnp.zeros((8, 128), F32)

    loads[0].wait()
    loads[1].wait()
    own_head = head[rows(256, m)]
    part_q[...] = jnp.dot(q_ref[...], own_head, preferred_element_type=F32).astype(BF)
    pl.semaphore_wait(barrier, len(peers))
    q1 = Send(part_q.at[rows(QM, osib)], rq.at[1], to_sib)
    q0 = Send(part_q.at[rows(QM, sib)], rq.at[0], to_sib)

    def head_rows(member, start, size):
        return head.at[pl.ds(pl.multiple_of(member * 256 + start, 32), size)]

    half_mine, half_other = 128 * (xi % 2), 128 * (1 - xi % 2)
    heads = []
    for j in range(4):
        mine = head_rows(m, half_mine + 32 * j, 32)
        heads.append(Send(mine, mine, to_back))
    near_head = Send(head_rows(m, 0, 256), head_rows(m, 0, 256), to_sib)
    q1.wait_recv()
    yq[...] = (part_q[rows(QM, opp)].astype(F32) + rq[1].astype(F32)).astype(BF)
    q2 = Send(yq, zq, to_opp)

    loads[2].wait()
    feature = rows(256, m)
    wide = [
        Send(p_ref.at[rows(256, core)], xh.at[:, feature], to_opp),
        Send(p_ref.at[rows(256, 1 - core)], xh.at[:, feature], to_osib),
        Send(p_ref.at[rows(256, 1 - core)], xh.at[:, feature], to_sib),
    ]
    xh[:, feature] = p_ref[rows(256, core)]
    side_heads, far_heads = [], []

    def pass_head(j):
        heads[j].wait_recv()
        theirs = head_rows(opp, half_mine + 32 * j, 32)
        side_heads.append(Send(theirs, theirs, at_x(1 if j % 2 == 0 else 3)))
        far_heads.append(Send(theirs, theirs, to_sib))


    def own_lanes(value):
        quarters = [value[:, k * QM : (k + 1) * QM] for k in range(4)]
        return jnp.where(
            m == 0, quarters[0],
            jnp.where(m == 1, quarters[1], jnp.where(m == 2, quarters[2], quarters[3])),
        )

    for copy in loads[3:]:
        copy.wait()
    count = counts_ref[slab]
    count_f = count.astype(F32)
    weight = own_lanes(weight_ref[...])
    slot = own_lanes(pos_ref[...].astype(F32))
    wanted = slot - count_f * jnp.floor((slot + 0.5) / count_f)
    auxs[...] = jnp.zeros_like(auxs)
    for k in range(5):
        auxs[k, 0:4, 0:QM] = own_lanes(mask_ref[k].astype(F32))
        auxs[k, 4:5, 0:QM] = weight
    xo[0:QM, rows(256, low)] = q_ref[rows(QM, m)]
    xo[QM:192, rows(256, low)] = p_ref[rows(PM, p_own)]
    xo[192 : 192 + QM, rows(256, low)] = q_ref[rows(QM, sib)]
    xo[192 + QM :, rows(256, low)] = p_ref[rows(PM, p_sib)]

    def normalise(projected):
        norm = jnp.sqrt(jnp.sum(projected * projected, axis=1, keepdims=True) + EPS)
        return projected / norm, norm

    pass_head(0)
    pass_head(1)
    q0.wait_recv()
    q2.wait_recv()
    unit, norm = normalise(
        part_q[rows(QM, m)].astype(F32) + rq[0].astype(F32) + zq[...].astype(F32)
    )
    unit_q[...] = unit
    norm_q[...] = norm
    qb[2 * QM : 3 * QM] = unit.astype(BF)
    def query_piece(k, h):
        return qb.at[(2 - k) * QM + h * 32 : (2 - k) * QM + (h + 1) * 32]

    queries, auxes = [], []
    for h in range(2):
        for k in (1, -1):
            queries.append(near_slab(query_piece(0, h), query_piece(k, h), k))
    for k in (1, -1, 2, -2):
        auxes.append(near_slab(auxs.at[2 + k], auxr.at[2 - k], k))

    def pass_on(h):
        for i, k in enumerate((1, -1)):
            queries[2 * h + i].wait_recv()
            further.append(
                Send(
                    query_piece(k, h), query_piece(2 * k, h), at_slab(k),
                    jnp.logical_and(inside(k), inside(-k)), inside(-2 * k),
                )
            )

    further = []
    pass_head(2)
    pass_head(3)
    wide_q = [
        Send(q_ref.at[rows(QM, member)], xo.at[first : first + QM, rows(256, low)], to_opp)
        for first, member in ((0, opp), (192, osib))
    ]

    def chip_part(chip):
        features = rows(512, chip)
        return jnp.dot(xh[:, features], head[features], preferred_element_type=F32)

    wide[2].wait_recv()
    near_head.wait_recv()
    projected = chip_part(low)
    for j in range(4):
        side_heads[j].wait_recv()
        theirs = head_rows(opp, half_other + 32 * j, 32)
        far_heads.append(Send(theirs, theirs, to_sib))
        if j % 2 == 1:
            pass_on(j // 2)
    for copy in wide[:2] + far_heads:
        copy.wait_recv()
    unit, norm = normalise(projected + chip_part(1 - low))
    unit_p[...] = unit
    norm_p[...] = norm
    pb[rows(256, core)] = unit.astype(BF)
    mine = pb.at[rows(256, core)]
    near = Send(mine, mine, to_sib)
    xo[QM:192, rows(256, 1 - low)] = xh[rows(PM, low), rows(256, opp)]
    wide_q.append(
        Send(xh.at[rows(PM, low), rows(256, osib)], xo.at[192 + QM : 384, rows(256, 1 - low)], to_sib)
    )
    near.wait_recv()
    for copy in further + auxes:
        copy.wait_recv()

    auxr[2] = auxs[2]
    for k in range(5):
        lanes = slice(k * QM, (k + 1) * QM)
        auxc[:, lanes] = auxr[k][:, 0:QM]
        auxc[5:6, lanes] = wanted if k == 2 else jnp.full((1, QM), -1.0, F32)
    scores = lax.dot_general(
        pb[...], qb[...], (((1,), (1,)), ((), ())), preferred_element_type=F32
    )
    slot_ids = lax.broadcasted_iota(jnp.int32, (PM, NQ), 0)
    others = jnp.zeros((1, NQ), F32)
    positive = jnp.zeros((1, NQ), F32)
    for tile in range(4):
        ids = slot_ids + tile * PM
        is_positive = ids.astype(F32) == auxc[5:6, :]
        kept = (ids < count) & (auxc[tile : tile + 1, :] > 0.5) & jnp.logical_not(is_positive)
        grown = jnp.exp(scores[tile * PM : (tile + 1) * PM] / TAU)
        terms = jnp.where(kept, grown, 0.0)
        others = others + jnp.sum(terms, axis=0, keepdims=True)
        positive = positive + jnp.sum(jnp.where(is_positive, grown, 0.0), axis=0, keepdims=True)
        ef[tile * PM : (tile + 1) * PM] = terms
        eb[tile * PM : (tile + 1) * PM] = terms.astype(BF)
    for k in range(5):
        tts[k // 2 : k // 2 + 1, (k % 2) * QM : (k % 2 + 1) * QM] = others[
            :, k * QM : (k + 1) * QM
        ]
    tts[2:3, QM:128] = positive[:, 2 * QM : 3 * QM]
    tts[3:4, :] = jnp.zeros((1, 128), F32)
    totals = [near_slab(tts, ttr.at[4 - k], k) for k in (1, -1, 2, -2, 3, -3, 4, -4)]

    terms = lax.dot_general(
        eb[...], pb[...], (((0,), (0,)), ((), ())), preferred_element_type=F32
    )
    returns = []
    for k in (2, -2, 1, -1):
        gs[2 + k] = terms[(2 + k) * QM : (3 + k) * QM].astype(BF)
        returns.append(near_slab(gs.at[2 + k], gr.at[2 - k], k))
    own_terms = terms[2 * QM : 3 * QM]

    ttr[4] = tts[...]
    for copy in totals:
        copy.wait_recv()
    for k in range(-2, 3):
        rest = jnp.zeros((1, QM), F32)
        for j in range(-2, 3):
            n = 2 - j
            rest = rest + ttr[k + j + 4][n // 2 : n // 2 + 1, (n % 2) * QM : (n % 2 + 1) * QM]
        whole = rest + ttr[k + 4][2:3, QM:128]
        lanes = slice((2 + k) * QM, (3 + k) * QM)
        scale = auxc[4:5, lanes] / (whole * TAU)
        auxc[6:7, lanes] = jnp.where(inside(k), scale, 0.0)
        if k == 0:
            own_rest, own_whole = rest, whole
            auxc[7:8, lanes] = scale * rest
        else:
            auxc[7:8, lanes] = jnp.zeros((1, QM), F32)

    def passage_terms(index):
        is_positive = (slot_ids + index * PM).astype(F32) == auxc[5:6, :]
        coefficient = jnp.where(is_positive, -auxc[7:8, :], ef[rows(PM, index)] * auxc[6:7, :])
        return jnp.dot(coefficient.astype(BF), qb[...], preferred_element_type=F32)

    pps[1] = passage_terms(p_osib).astype(BF)
    pieces = [slice(0, 64), slice(64, 128)]
    p1 = [Send(pps.at[1, piece], pr.at[1, piece], to_sib) for piece in pieces]
    part = passage_terms(p_opp)
    p2 = []
    for copy, piece in zip(p1, pieces):
        copy.wait_recv()
        py[piece] = (part[piece] + pr[1, piece].astype(F32)).astype(BF)
        p2.append(Send(py.at[piece], pz.at[piece], to_opp))
    pps[0] = passage_terms(p_sib).astype(BF)
    p0 = Send(pps.at[0], pr.at[0], to_sib)
    own_part = passage_terms(p_own)

    def tangent(unit, norm, grad):
        radial = jnp.sum(unit * grad, axis=1, keepdims=True)
        return ((grad - unit * radial) / norm).astype(BF)

    eye = lax.broadcasted_iota(jnp.int32, (QM, QM), 0) == lax.broadcasted_iota(
        jnp.int32, (QM, QM), 1
    )

    def column(row):
        return jnp.sum(jnp.where(eye, row, 0.0), axis=1, keepdims=True)

    one_hot = (
        lax.broadcasted_iota(jnp.int32, (4 * PM, QM), 0).astype(F32) == wanted
    ).astype(F32).astype(BF)
    chosen = lax.dot_general(
        one_hot, pb[...], (((0,), (0,)), ((), ())), preferred_element_type=F32
    )
    scale = column(weight / (own_whole * TAU))
    drop = column(weight * own_rest / (own_whole * TAU))
    for copy in returns:
        copy.wait_recv()
    for k in (0, 1, 3, 4):
        own_terms = own_terms + gr[k].astype(F32)
    pgt[0:QM] = tangent(unit_q[...], norm_q[...], own_terms * scale - chosen * drop)
    shared = [Send(pgt.at[0:QM], pgt.at[192 : 192 + QM], to_sib)]
    for copy in [p0] + p2:
        copy.wait_recv()
    summed = own_part + pr[0].astype(F32) + pz[...].astype(F32)
    pgt[QM:192] = tangent(unit_p[rows(PM, low)], norm_p[rows(PM, low)], summed)
    shared.append(Send(pgt.at[QM:192], pgt.at[192 + QM : 384], to_sib))

    def cols(size, index):
        return pl.ds(pl.multiple_of(index * size, size), size)

    for copy in wide_q + shared:
        copy.wait_recv()

    first = []
    for half in range(2):
        there = slice(half * 128, (half + 1) * 128)
        for block in range(2):
            features = slice(block * 256 + half * 128, block * 256 + (half + 1) * 128)
            total = lax.dot_general(
                xo[:, features], pgt[...], (((0,), (0,)), ((), ())), preferred_element_type=F32
            )
            hf[block, there] = total
            hb[block, there] = total.astype(BF)
        if half == 0:
            for k in (2, 1, 3):
                first.append(
                    Send(hb.at[:, there, cols(256, (xi + k) % 4)], ax.at[k - 1], at_x(k))
                )
        else:
            first.append(Send(hb.at[low, there, cols(512, 1 - high)], cy.at[2], to_high))
            first.append(Send(hb.at[1 - low, there, cols(512, high)], cy.at[0], to_opp))
            first.append(Send(hb.at[1 - low, there, cols(512, 1 - high)], cy.at[1], to_back))

    eo[...] = lax.dot_general(
        pgt[0:192], head[...], (((1,), (1,)), ((), ())), preferred_element_type=F32
    ).astype(BF)
    oq_ref[rows(QM, m)] = eo[0:QM, cols(256, m)]
    op_ref[rows(PM, p_own)] = eo[QM:, cols(256, m)]

    def spread(member, device):
        return [
            Send(eo.at[0:QM, cols(256, member)], oq_ref.at[rows(QM, m)], device),
            Send(eo.at[QM : QM + PM, cols(256, member)], op_ref.at[rows(PM, p_own)], device),
        ]

    outs = spread(sib, to_sib)

    for copy in first[:3]:
        copy.wait_recv()
    total = hf[:, 0:128, cols(256, xi)]
    for k in range(3):
        total = total + ax[k].astype(F32)
    a1f[...] = total
    a1[...] = total.astype(BF)
    second = [
        Send(a1.at[low, :, cols(128, 1 - high)], ay.at[2], to_high),
        Send(a1.at[1 - low, :, cols(128, high)], ay.at[0], to_opp),
        Send(a1.at[1 - low, :, cols(128, 1 - high)], ay.at[1], to_back),
    ]
    for copy in first[3:]:
        copy.wait_recv()
    total = hf[low, 128:256, cols(512, high)]
    for k in range(3):
        total = total + cy[k].astype(F32)
    c1f[...] = total
    c1[...] = total.astype(BF)
    for k in (2, 1, 3):
        second.append(Send(c1.at[:, cols(128, (xi + k) % 4)], cx.at[k - 1], at_x(k)))
    for copy in second:
        copy.wait_recv()
    total = a1f[low, :, cols(128, high)]
    for k in range(3):
        total = total + ay[k].astype(F32)
    e1f[0:128] = total
    e1[0:128] = total.astype(BF)
    total = c1f[:, cols(128, xi)]
    for k in range(3):
        total = total + cx[k].astype(F32)
    e1f[128:256] = total
    e1[128:256] = total.astype(BF)
    third = []
    for k in (4, 3, 5, 2, 6, 1, 7):
        third.append(Send(e1.at[rows(32, (zi + k) % 8)], ez.at[k - 1], at_z(k)))
    outs += spread(opp, to_opp) + spread(osib, to_osib)
    for copy in third:
        copy.wait_recv()
    total = e1f[rows(32, zi)]
    for k in range(7):
        total = total + ez[k].astype(F32)
    gz[rows(32, zi)] = total.astype(BF)
    fourth = []
    for k in (4, 3, 5, 2, 6, 1, 7):
        fourth.append(Send(gz.at[rows(32, zi)], gz.at[rows(32, zi)], at_z(k)))
    for copy in fourth:
        copy.wait_recv()
    own = high * 4 + xi
    last = [Send(gz, ga.at[own], at_high_x(k)) for k in (2, 1, 3)]
    last += [Send(gz, ga.at[own], at_x(k)) for k in (2, 1, 3)]
    last.append(Send(gz, ga.at[own], to_high))
    ga[own] = gz[...]
    for copy in outs + last:
        copy.wait_recv()
    for j in range(8):
        upper, lower = 2 * (j % 4) + j // 4, j
        oh_ref[0:128, upper * 128 : (upper + 1) * 128] = ga[j, 0:128]
        oh_ref[128:256, lower * 128 : (lower + 1) * 128] = ga[j, 128:256]
    for copy in sent:
        copy.wait_send()


def body(query_emb, passage_emb, head, fn_mask, counts, positive_slot, query_weight):
    vmem = pl.BlockSpec(memory_space=pltpu.VMEM)
    hbm = pl.BlockSpec(memory_space=pltpu.HBM)

    def half(*shape):
        return pltpu.VMEM(shape, BF)

    def full(*shape):
        return pltpu.VMEM(shape, F32)

    query_grad, passage_grad, head_grad = pl.pallas_call(
        kernel,
        out_shape=(
            jax.ShapeDtypeStruct((256, 256), BF),
            jax.ShapeDtypeStruct((512, 256), BF),
            jax.ShapeDtypeStruct((256, D), BF),
        ),
        in_specs=[hbm] * 7,
        out_specs=(vmem, vmem, vmem),
        scratch_shapes=[
            half(256, 256), half(512, 256), half(D, D),
            pltpu.VMEM((5, 4, 256), jnp.int32), pltpu.SMEM((64,), jnp.int32),
            pltpu.VMEM((1, 256), jnp.int32), full(1, 256),
            half(256, D), half(2, QM, D), half(QM, D), half(QM, D), half(256, D),
            full(QM, D), full(256, D), full(QM, 1), full(256, 1),
            half(NQ, D), half(4 * PM, D), full(5, 8, 128), full(5, 8, 128), full(8, NQ),
            full(4 * PM, NQ), half(4 * PM, NQ), full(4, 128), full(9, 4, 128),
            half(5, QM, D), half(5, QM, D),
            half(2, PM, D), half(2, PM, D), half(PM, D), half(PM, D),
            half(384, 512), half(384, D), half(192, D),
            full(2, 256, D), half(2, 256, D),
            half(3, 2, 128, 256), half(3, 128, 512),
            full(2, 128, 256), full(128, 512), half(2, 128, 256), half(128, 512),
            half(3, 128, 128), half(3, 128, 128), full(256, 128), half(256, 128),
            half(7, 32, 128), half(256, 128), half(8, 256, 128),
            pltpu.SemaphoreType.DMA((7,)),
            pltpu.SemaphoreType.DMA((SEMS,)), pltpu.SemaphoreType.DMA((SEMS,)),
        ],
        compiler_params=pltpu.CompilerParams(
            collective_id=0, has_side_effects=True, vmem_limit_bytes=48 << 20
        ),
        cost_estimate=pl.CostEstimate(flops=3 << 30, bytes_accessed=4 << 20, transcendentals=0),
    )(*[
        pltpu.with_memory_space_constraint(value, pltpu.HBM)
        for value in (
            query_emb, passage_emb, head, jnp.transpose(fn_mask, (1, 2, 0)), counts,
            positive_slot.reshape(1, -1), query_weight.reshape(1, -1),
        )
    ])
    return query_grad, passage_grad, head_grad.astype(F32)


def solution(mesh):
    return jax.shard_map(
        body,
        mesh=mesh,
        in_specs=(
            P("slab", "mp"), P("slab", "mp"), P("mp", None), P("slab", None, None),
            P(), P("slab"), P("slab"),
        ),
        out_specs=(P("slab", "mp"), P("slab", "mp"), P("mp", None)),
        check_vma=False,
    )
```

```python
import jax
import jax.numpy as jnp
from jax import lax
from jax.experimental import pallas as pl
from jax.experimental.pallas import tpu as pltpu
from jax.sharding import PartitionSpec as P

EPS = 1e-06
TAU = 0.05
D = 1024
QM = 64
PM = 128
NQ = 5 * QM
SEMS = 176
MESH = pl.DeviceIdType.MESH
BF = jnp.bfloat16
F32 = jnp.float32


def kernel(
    q_hbm, p_hbm, head_hbm, mask_hbm, counts_hbm, pos_hbm, weight_hbm,
    oq_ref, op_ref, oh_ref,
    q_ref, p_ref, head, mask_ref, counts_ref, pos_ref, weight_ref,
    part_q, rq, yq, zq, xh, unit_q, unit_p, norm_q, norm_p,
    qb, pb, auxs, auxr, auxc, ef, eb, tts, ttr, gs, gr,
    pps, pr, py, pz, xo, pgt, eo,
    hf, hb, ax, cy, a1f, c1f, a1, c1, ay, cx, e1f, e1, ez, gz, ga,
    lsem, ssem, rsem,
):
    slab = lax.axis_index("slab")
    m = lax.axis_index("mp")
    core, low = m % 2, m // 2
    sib = 2 * low + 1 - core
    opp = 2 * (1 - low) + core
    osib = 2 * (1 - low) + 1 - core
    high, xi, zi = slab // 32, (slab // 8) % 4, slab % 8
    p_own, p_sib = 2 * core + low, 2 * (1 - core) + low
    p_opp, p_osib = 2 * core + 1 - low, 2 * (1 - core) + 1 - low

    def at_slab(distance):
        there = (slab + distance + 64) % 64
        return (there, jnp.where(there // 32 == high, m, opp))

    def at_x(step):
        return (high * 32 + ((xi + step) % 4) * 8 + zi, m)

    def at_high_x(step):
        return ((1 - high) * 32 + ((xi + step) % 4) * 8 + zi, m)

    def at_z(step):
        return (high * 32 + xi * 8 + (zi + step) % 8, m)

    def inside(distance):
        return jnp.logical_and(slab + distance >= 0, slab + distance < 64)

    to_sib, to_opp, to_osib = (slab, sib), (slab, opp), (slab, osib)
    to_high, to_back = ((slab + 32) % 64, m), ((slab + 32) % 64, opp)
    peers = [to_sib, to_opp, to_osib, to_high, to_back]
    peers += [at_slab(k) for k in (-4, -3, -2, -1, 1, 2, 3, 4)]
    peers += [at_x(k) for k in range(1, 4)] + [at_z(k) for k in range(1, 8)]
    peers += [at_high_x(k) for k in range(1, 4)]
    sent = []

    class Send:
        def __init__(self, src, dst, device, leaves=None, comes=None):
            i = len(sent)
            self.copy = pltpu.make_async_remote_copy(
                src_ref=src, dst_ref=dst, send_sem=ssem.at[i], recv_sem=rsem.at[i],
                device_id=device, device_id_type=MESH,
            )
            self.leaves, self.comes = leaves, comes
            self.act(leaves, self.copy.start)
            sent.append(self)

        def act(self, condition, action):
            if condition is None:
                action()
            else:
                pl.when(condition)(action)

        def wait_recv(self):
            self.act(self.comes, self.copy.wait_recv)

        def wait_send(self):
            self.act(self.leaves, self.copy.wait_send)

    def near_slab(src, dst, distance):
        return Send(src, dst, at_slab(distance), inside(distance), inside(-distance))

    def rows(count, index):
        return pl.ds(pl.multiple_of(count * index, count), count)

    barrier = pltpu.get_barrier_semaphore()
    for peer in peers:
        pl.semaphore_signal(barrier, inc=1, device_id=peer, device_id_type=MESH)
    loads = [
        pltpu.make_async_copy(src, dst, lsem.at[i])
        for i, (src, dst) in enumerate((
            (q_hbm, q_ref), (head_hbm, head.at[rows(256, m)]), (p_hbm, p_ref),
            (mask_hbm, mask_ref), (counts_hbm, counts_ref), (pos_hbm, pos_ref),
            (weight_hbm, weight_ref),
        ))
    ]
    for copy in loads:
        copy.start()

    for k in (-4, -3, -2, -1, 1, 2, 3, 4):
        @pl.when(jnp.logical_not(inside(k)))
        def _():
            ttr[k + 4] = jnp.zeros((4, 128), F32)
            if abs(k) <= 2:
                qb[(2 + k) * QM : (3 + k) * QM] = jnp.zeros((QM, D), BF)
                gr[k + 2] = jnp.zeros((QM, D), BF)
                auxr[k + 2] = jnp.zeros((8, 128), F32)

    loads[0].wait()
    loads[1].wait()
    own_head = head[rows(256, m)]
    part_q[...] = jnp.dot(q_ref[...], own_head, preferred_element_type=F32).astype(BF)
    pl.semaphore_wait(barrier, len(peers))
    q1 = Send(part_q.at[rows(QM, osib)], rq.at[1], to_sib)
    q0 = Send(part_q.at[rows(QM, sib)], rq.at[0], to_sib)

    def head_rows(member, start, size):
        return head.at[pl.ds(pl.multiple_of(member * 256 + start, 32), size)]

    half_mine, half_other = 128 * (xi % 2), 128 * (1 - xi % 2)
    heads = []
    for j in range(4):
        mine = head_rows(m, half_mine + 32 * j, 32)
        heads.append(Send(mine, mine, to_back))
    near_head = Send(head_rows(m, 0, 256), head_rows(m, 0, 256), to_sib)
    q1.wait_recv()
    yq[...] = (part_q[rows(QM, opp)].astype(F32) + rq[1].astype(F32)).astype(BF)
    q2 = Send(yq, zq, to_opp)

    loads[2].wait()
    feature = rows(256, m)
    wide = [
        Send(p_ref.at[rows(256, core)], xh.at[:, feature], to_opp),
        Send(p_ref.at[rows(256, 1 - core)], xh.at[:, feature], to_osib),
        Send(p_ref.at[rows(256, 1 - core)], xh.at[:, feature], to_sib),
    ]
    xh[:, feature] = p_ref[rows(256, core)]
    side_heads, far_heads = [], []

    def pass_head(j):
        heads[j].wait_recv()
        theirs = head_rows(opp, half_mine + 32 * j, 32)
        side_heads.append(Send(theirs, theirs, at_x(1 if j % 2 == 0 else 3)))
        far_heads.append(Send(theirs, theirs, to_sib))


    def own_lanes(value):
        quarters = [value[:, k * QM : (k + 1) * QM] for k in range(4)]
        return jnp.where(
            m == 0, quarters[0],
            jnp.where(m == 1, quarters[1], jnp.where(m == 2, quarters[2], quarters[3])),
        )

    for copy in loads[3:]:
        copy.wait()
    count = counts_ref[slab]
    count_f = count.astype(F32)
    weight = own_lanes(weight_ref[...])
    slot = own_lanes(pos_ref[...].astype(F32))
    wanted = slot - count_f * jnp.floor((slot + 0.5) / count_f)
    auxs[...] = jnp.zeros_like(auxs)
    for k in range(5):
        auxs[k, 0:4, 0:QM] = own_lanes(mask_ref[k].astype(F32))
        auxs[k, 4:5, 0:QM] = weight
    xo[0:QM, rows(256, low)] = q_ref[rows(QM, m)]
    xo[QM:192, rows(256, low)] = p_ref[rows(PM, p_own)]
    xo[192 : 192 + QM, rows(256, low)] = q_ref[rows(QM, sib)]
    xo[192 + QM :, rows(256, low)] = p_ref[rows(PM, p_sib)]

    def normalise(projected):
        norm = jnp.sqrt(jnp.sum(projected * projected, axis=1, keepdims=True) + EPS)
        return projected / norm, norm

    pass_head(0)
    pass_head(1)
    q0.wait_recv()
    q2.wait_recv()
    unit, norm = normalise(
        part_q[rows(QM, m)].astype(F32) + rq[0].astype(F32) + zq[...].astype(F32)
    )
    unit_q[...] = unit
    norm_q[...] = norm
    qb[2 * QM : 3 * QM] = unit.astype(BF)
    def query_piece(k, h):
        return qb.at[(2 - k) * QM + h * 32 : (2 - k) * QM + (h + 1) * 32]

    queries, auxes = [], []
    for h in range(2):
        for k in (1, -1):
            queries.append(near_slab(query_piece(0, h), query_piece(k, h), k))
    for k in (1, -1, 2, -2):
        auxes.append(near_slab(auxs.at[2 + k], auxr.at[2 - k], k))

    def pass_on(h):
        for i, k in enumerate((1, -1)):
            queries[2 * h + i].wait_recv()
            further.append(
                Send(
                    query_piece(k, h), query_piece(2 * k, h), at_slab(k),
                    jnp.logical_and(inside(k), inside(-k)), inside(-2 * k),
                )
            )

    further = []
    pass_head(2)
    pass_head(3)
    wide_q = [
        Send(q_ref.at[rows(QM, member)], xo.at[first : first + QM, rows(256, low)], to_opp)
        for first, member in ((0, opp), (192, osib))
    ]

    def chip_part(chip):
        features = rows(512, chip)
        return jnp.dot(xh[:, features], head[features], preferred_element_type=F32)

    wide[2].wait_recv()
    near_head.wait_recv()
    projected = chip_part(low)
    for j in range(4):
        side_heads[j].wait_recv()
        theirs = head_rows(opp, half_other + 32 * j, 32)
        far_heads.append(Send(theirs, theirs, to_sib))
        if j % 2 == 1:
            pass_on(j // 2)
    for copy in wide[:2] + far_heads:
        copy.wait_recv()
    unit, norm = normalise(projected + chip_part(1 - low))
    unit_p[...] = unit
    norm_p[...] = norm
    pb[rows(256, core)] = unit.astype(BF)
    mine = pb.at[rows(256, core)]
    near = Send(mine, mine, to_sib)
    xo[QM:192, rows(256, 1 - low)] = xh[rows(PM, low), rows(256, opp)]
    wide_q.append(
        Send(xh.at[rows(PM, low), rows(256, osib)], xo.at[192 + QM : 384, rows(256, 1 - low)], to_sib)
    )
    near.wait_recv()
    for copy in further + auxes:
        copy.wait_recv()

    auxr[2] = auxs[2]
    for k in range(5):
        lanes = slice(k * QM, (k + 1) * QM)
        auxc[:, lanes] = auxr[k][:, 0:QM]
        auxc[5:6, lanes] = wanted if k == 2 else jnp.full((1, QM), -1.0, F32)
    scores = lax.dot_general(
        pb[...], qb[...], (((1,), (1,)), ((), ())), preferred_element_type=F32
    )
    slot_ids = lax.broadcasted_iota(jnp.int32, (PM, NQ), 0)
    others = jnp.zeros((1, NQ), F32)
    positive = jnp.zeros((1, NQ), F32)
    for tile in range(4):
        ids = slot_ids + tile * PM
        is_positive = ids.astype(F32) == auxc[5:6, :]
        kept = (ids < count) & (auxc[tile : tile + 1, :] > 0.5) & jnp.logical_not(is_positive)
        grown = jnp.exp(scores[tile * PM : (tile + 1) * PM] / TAU)
        terms = jnp.where(kept, grown, 0.0)
        others = others + jnp.sum(terms, axis=0, keepdims=True)
        positive = positive + jnp.sum(jnp.where(is_positive, grown, 0.0), axis=0, keepdims=True)
        ef[tile * PM : (tile + 1) * PM] = terms
        eb[tile * PM : (tile + 1) * PM] = terms.astype(BF)
    for k in range(5):
        tts[k // 2 : k // 2 + 1, (k % 2) * QM : (k % 2 + 1) * QM] = others[
            :, k * QM : (k + 1) * QM
        ]
    tts[2:3, QM:128] = positive[:, 2 * QM : 3 * QM]
    tts[3:4, :] = jnp.zeros((1, 128), F32)
    totals = [near_slab(tts, ttr.at[4 - k], k) for k in (1, -1, 2, -2, 3, -3, 4, -4)]

    terms = lax.dot_general(
        eb[...], pb[...], (((0,), (0,)), ((), ())), preferred_element_type=F32
    )
    returns = []
    for k in (2, -2, 1, -1):
        gs[2 + k] = terms[(2 + k) * QM : (3 + k) * QM].astype(BF)
        returns.append(near_slab(gs.at[2 + k], gr.at[2 - k], k))
    own_terms = terms[2 * QM : 3 * QM]

    ttr[4] = tts[...]
    for copy in totals:
        copy.wait_recv()
    for k in range(-2, 3):
        rest = jnp.zeros((1, QM), F32)
        for j in range(-2, 3):
            n = 2 - j
            rest = rest + ttr[k + j + 4][n // 2 : n // 2 + 1, (n % 2) * QM : (n % 2 + 1) * QM]
        whole = rest + ttr[k + 4][2:3, QM:128]
        lanes = slice((2 + k) * QM, (3 + k) * QM)
        scale = auxc[4:5, lanes] / (whole * TAU)
        auxc[6:7, lanes] = jnp.where(inside(k), scale, 0.0)
        if k == 0:
            own_rest, own_whole = rest, whole
            auxc[7:8, lanes] = scale * rest
        else:
            auxc[7:8, lanes] = jnp.zeros((1, QM), F32)

    def passage_terms(index):
        is_positive = (slot_ids + index * PM).astype(F32) == auxc[5:6, :]
        coefficient = jnp.where(is_positive, -auxc[7:8, :], ef[rows(PM, index)] * auxc[6:7, :])
        return jnp.dot(coefficient.astype(BF), qb[...], preferred_element_type=F32)

    pps[1] = passage_terms(p_osib).astype(BF)
    pieces = [slice(0, 64), slice(64, 128)]
    p1 = [Send(pps.at[1, piece], pr.at[1, piece], to_sib) for piece in pieces]
    part = passage_terms(p_opp)
    p2 = []
    for copy, piece in zip(p1, pieces):
        copy.wait_recv()
        py[piece] = (part[piece] + pr[1, piece].astype(F32)).astype(BF)
        p2.append(Send(py.at[piece], pz.at[piece], to_opp))
    pps[0] = passage_terms(p_sib).astype(BF)
    p0 = Send(pps.at[0], pr.at[0], to_sib)
    own_part = passage_terms(p_own)

    def tangent(unit, norm, grad):
        radial = jnp.sum(unit * grad, axis=1, keepdims=True)
        return ((grad - unit * radial) / norm).astype(BF)

    eye = lax.broadcasted_iota(jnp.int32, (QM, QM), 0) == lax.broadcasted_iota(
        jnp.int32, (QM, QM), 1
    )

    def column(row):
        return jnp.sum(jnp.where(eye, row, 0.0), axis=1, keepdims=True)

    one_hot = (
        lax.broadcasted_iota(jnp.int32, (4 * PM, QM), 0).astype(F32) == wanted
    ).astype(F32).astype(BF)
    chosen = lax.dot_general(
        one_hot, pb[...], (((0,), (0,)), ((), ())), preferred_element_type=F32
    )
    scale = column(weight / (own_whole * TAU))
    drop = column(weight * own_rest / (own_whole * TAU))
    for copy in returns:
        copy.wait_recv()
    for k in (0, 1, 3, 4):
        own_terms = own_terms + gr[k].astype(F32)
    pgt[0:QM] = tangent(unit_q[...], norm_q[...], own_terms * scale - chosen * drop)
    shared = [Send(pgt.at[0:QM], pgt.at[192 : 192 + QM], to_sib)]
    p0.wait_recv()
    for i, piece in enumerate(pieces):
        p2[i].wait_recv()
        there = slice(QM + 64 * i, QM + 64 * (i + 1))
        line = pl.ds(pl.multiple_of(PM * low + 64 * i, 64), 64)
        summed = own_part[piece] + pr[0, piece].astype(F32) + pz[piece].astype(F32)
        pgt[there] = tangent(unit_p[line], norm_p[line], summed)
        shared.append(
            Send(pgt.at[there], pgt.at[192 + QM + 64 * i : 192 + QM + 64 * (i + 1)], to_sib)
        )

    def cols(size, index):
        return pl.ds(pl.multiple_of(index * size, size), size)

    for copy in wide_q + shared:
        copy.wait_recv()

    first, second, third, fourth, last = ([[], []] for _ in range(5))

    def term(half):
        features = jnp.concatenate(
            [xo[:, k + half * 128 : k + (half + 1) * 128] for k in (0, 256)], axis=1
        )
        total = lax.dot_general(
            features, pgt[...], (((0,), (0,)), ((), ())), preferred_element_type=F32
        )
        there = slice(half * 128, (half + 1) * 128)
        for block in range(2):
            hf[block, there] = total[block * 128 : (block + 1) * 128]
            hb[block, there] = total[block * 128 : (block + 1) * 128].astype(BF)

    term(0)
    for s in range(2):
        there = slice(64 * s, 64 * (s + 1))
        for k in (2, 1, 3):
            first[s].append(
                Send(hb.at[:, there, cols(256, (xi + k) % 4)], ax.at[s, k - 1], at_x(k))
            )
    term(1)
    for s in range(2):
        there = slice(128 + 64 * s, 128 + 64 * (s + 1))
        first[s] += [
            Send(hb.at[low, there, cols(512, 1 - high)], cy.at[s, 2], to_high),
            Send(hb.at[1 - low, there, cols(512, high)], cy.at[s, 0], to_opp),
            Send(hb.at[1 - low, there, cols(512, 1 - high)], cy.at[s, 1], to_back),
        ]

    eo[...] = lax.dot_general(
        pgt[0:192], head[...], (((1,), (1,)), ((), ())), preferred_element_type=F32
    ).astype(BF)
    oq_ref[rows(QM, m)] = eo[0:QM, cols(256, m)]
    op_ref[rows(PM, p_own)] = eo[QM:, cols(256, m)]

    def spread(member, device):
        return [
            Send(eo.at[0:QM, cols(256, member)], oq_ref.at[rows(QM, m)], device),
            Send(eo.at[QM : QM + PM, cols(256, member)], op_ref.at[rows(PM, p_own)], device),
        ]

    outs = spread(sib, to_sib)

    def plus(total, ref, s, count):
        for k in range(count):
            total = total + ref[s, k].astype(F32)
        return total

    def along_second(s):
        for copy in first[s][:3]:
            copy.wait_recv()
        total = plus(hf[:, 64 * s : 64 * (s + 1), cols(256, xi)], ax, s, 3)
        a1f[s] = total
        a1[s] = total.astype(BF)
        second[s] += [
            Send(a1.at[s, low, :, cols(128, 1 - high)], ay.at[s, 2], to_high),
            Send(a1.at[s, 1 - low, :, cols(128, high)], ay.at[s, 0], to_opp),
            Send(a1.at[s, 1 - low, :, cols(128, 1 - high)], ay.at[s, 1], to_back),
        ]
        for copy in first[s][3:]:
            copy.wait_recv()
        total = plus(hf[low, 128 + 64 * s : 128 + 64 * (s + 1), cols(512, high)], cy, s, 3)
        c1f[s] = total
        c1[s] = total.astype(BF)
        for k in (2, 1, 3):
            second[s].append(
                Send(c1.at[s, :, cols(128, (xi + k) % 4)], cx.at[s, k - 1], at_x(k))
            )

    def along_z(s):
        for copy in second[s]:
            copy.wait_recv()
        total = plus(a1f[s, low, :, cols(128, high)], ay, s, 3)
        e1f[s, 0:64] = total
        e1[s, 0:64] = total.astype(BF)
        total = plus(c1f[s, :, cols(128, xi)], cx, s, 3)
        e1f[s, 64:128] = total
        e1[s, 64:128] = total.astype(BF)
        for k in (4, 3, 5, 2, 6, 1, 7):
            third[s].append(Send(e1.at[s, rows(16, (zi + k) % 8)], ez.at[s, k - 1], at_z(k)))

    def back_z(s):
        for copy in third[s]:
            copy.wait_recv()
        mine = gz.at[s, rows(16, zi)]
        mine[...] = plus(e1f[s, rows(16, zi)], ez, s, 7).astype(BF)
        for k in (4, 3, 5, 2, 6, 1, 7):
            fourth[s].append(Send(mine, mine, at_z(k)))

    own = high * 4 + xi

    def back(s):
        for copy in fourth[s]:
            copy.wait_recv()
        last[s] += [Send(gz.at[s], ga.at[s, own], at_high_x(k)) for k in (2, 1, 3)]
        last[s] += [Send(gz.at[s], ga.at[s, own], at_x(k)) for k in (2, 1, 3)]
        last[s].append(Send(gz.at[s], ga.at[s, own], to_high))
        ga[s, own] = gz[s]

    along_second(0)
    along_second(1)
    along_z(0)
    along_z(1)
    outs += spread(opp, to_opp) + spread(osib, to_osib)
    back_z(0)
    back_z(1)
    back(0)
    back(1)
    for s in range(2):
        for copy in last[s]:
            copy.wait_recv()
        for j in range(8):
            upper, lower = 128 * (2 * (j % 4) + j // 4), 128 * j
            oh_ref[64 * s : 64 * (s + 1), upper : upper + 128] = ga[s, j, 0:64]
            oh_ref[128 + 64 * s : 128 + 64 * (s + 1), lower : lower + 128] = ga[s, j, 64:128]
    for copy in outs:
        copy.wait_recv()
    for copy in sent:
        copy.wait_send()


def emit(query, passage, term, query_out, passage_out, head_out, wide, sems):
    copies = [
        pltpu.make_async_copy(query, query_out, sems.at[0]),
        pltpu.make_async_copy(passage, passage_out, sems.at[1]),
    ]
    for copy in copies:
        copy.start()
    for part in range(2):
        there = slice(part * 128, (part + 1) * 128)
        wide[there] = term[there].astype(F32)
        copies.append(
            pltpu.make_async_copy(wide.at[there], head_out.at[there], sems.at[2 + part])
        )
        copies[-1].start()
    for copy in copies:
        copy.wait()


def body(query_emb, passage_emb, head, fn_mask, counts, positive_slot, query_weight):
    vmem = pl.BlockSpec(memory_space=pltpu.VMEM)
    hbm = pl.BlockSpec(memory_space=pltpu.HBM)

    def half(*shape):
        return pltpu.VMEM(shape, BF)

    def full(*shape):
        return pltpu.VMEM(shape, F32)

    grads = pl.pallas_call(
        kernel,
        out_shape=(
            jax.ShapeDtypeStruct((256, 256), BF),
            jax.ShapeDtypeStruct((512, 256), BF),
            jax.ShapeDtypeStruct((256, D), BF),
        ),
        in_specs=[hbm] * 7,
        out_specs=(vmem, vmem, vmem),
        scratch_shapes=[
            half(256, 256), half(512, 256), half(D, D),
            pltpu.VMEM((5, 4, 256), jnp.int32), pltpu.SMEM((64,), jnp.int32),
            pltpu.VMEM((1, 256), jnp.int32), full(1, 256),
            half(256, D), half(2, QM, D), half(QM, D), half(QM, D), half(256, D),
            full(QM, D), full(256, D), full(QM, 1), full(256, 1),
            half(NQ, D), half(4 * PM, D), full(5, 8, 128), full(5, 8, 128), full(8, NQ),
            full(4 * PM, NQ), half(4 * PM, NQ), full(4, 128), full(9, 4, 128),
            half(5, QM, D), half(5, QM, D),
            half(2, PM, D), half(2, PM, D), half(PM, D), half(PM, D),
            half(384, 512), half(384, D), half(192, D),
            full(2, 256, D), half(2, 256, D),
            half(2, 3, 2, 64, 256), half(2, 3, 64, 512),
            full(2, 2, 64, 256), full(2, 64, 512), half(2, 2, 64, 256), half(2, 64, 512),
            half(2, 3, 64, 128), half(2, 3, 64, 128), full(2, 128, 128), half(2, 128, 128),
            half(2, 7, 16, 128), half(2, 128, 128), half(2, 8, 128, 128),
            pltpu.SemaphoreType.DMA((7,)),
            pltpu.SemaphoreType.DMA((SEMS,)), pltpu.SemaphoreType.DMA((SEMS,)),
        ],
        compiler_params=pltpu.CompilerParams(
            collective_id=0, has_side_effects=True, vmem_limit_bytes=48 << 20
        ),
        cost_estimate=pl.CostEstimate(flops=3 << 30, bytes_accessed=4 << 20, transcendentals=0),
    )(*[
        pltpu.with_memory_space_constraint(value, pltpu.HBM)
        for value in (
            query_emb, passage_emb, head, jnp.transpose(fn_mask, (1, 2, 0)), counts,
            positive_slot.reshape(1, -1), query_weight.reshape(1, -1),
        )
    ])
    return pl.pallas_call(
        emit,
        out_shape=(
            jax.ShapeDtypeStruct((256, 256), BF),
            jax.ShapeDtypeStruct((512, 256), BF),
            jax.ShapeDtypeStruct((256, D), F32),
        ),
        in_specs=[vmem] * 3,
        out_specs=(hbm,) * 3,
        scratch_shapes=[full(256, D), pltpu.SemaphoreType.DMA((4,))],
        compiler_params=pltpu.CompilerParams(vmem_limit_bytes=8 << 20),
    )(*grads)


def solution(mesh):
    return jax.shard_map(
        body,
        mesh=mesh,
        in_specs=(
            P("slab", "mp"), P("slab", "mp"), P("mp", None), P("slab", None, None),
            P(), P("slab"), P("slab"),
        ),
        out_specs=(P("slab", "mp"), P("slab", "mp"), P("mp", None)),
        check_vma=False,
    )
```

```python
import jax
import jax.numpy as jnp
from jax import lax
from jax.experimental import pallas as pl
from jax.experimental.pallas import tpu as pltpu
from jax.sharding import PartitionSpec as P

EPS = 1e-06
TAU = 0.05
D = 1024
QM = 64
PM = 128
NQ = 5 * QM
SEMS = 176
MESH = pl.DeviceIdType.MESH
BF = jnp.bfloat16
F32 = jnp.float32


def kernel(
    q_hbm, p_hbm, head_hbm, mask_hbm, counts_hbm, pos_hbm, weight_hbm,
    oq_ref, op_ref, oh_ref,
    q_ref, p_ref, head, mask_ref, counts_ref, pos_ref, weight_ref,
    part_q, rq, yq, zq, xh, unit_q, unit_p, norm_q, norm_p,
    qb, pb, auxs, auxr, auxc, ef, eb, tts, ttr, gs, gr,
    pps, pr, py, pz, xo, pgt, eo,
    hf, hb, ax, cy, a1f, c1f, a1, c1, ay, cx, e1f, e1, ez, gz, ga,
    lsem, ssem, rsem,
):
    slab = lax.axis_index("slab")
    m = lax.axis_index("mp")
    core, low = m % 2, m // 2
    sib = 2 * low + 1 - core
    opp = 2 * (1 - low) + core
    osib = 2 * (1 - low) + 1 - core
    high, xi, zi = slab // 32, (slab // 8) % 4, slab % 8
    p_own, p_sib = 2 * core + low, 2 * (1 - core) + low
    p_opp, p_osib = 2 * core + 1 - low, 2 * (1 - core) + 1 - low

    def at_slab(distance):
        there = (slab + distance + 64) % 64
        return (there, jnp.where(there // 32 == high, m, opp))

    def at_x(step):
        return (high * 32 + ((xi + step) % 4) * 8 + zi, m)

    def at_high_x(step):
        return ((1 - high) * 32 + ((xi + step) % 4) * 8 + zi, m)

    def at_z(step):
        return (high * 32 + xi * 8 + (zi + step) % 8, m)

    def inside(distance):
        return jnp.logical_and(slab + distance >= 0, slab + distance < 64)

    to_sib, to_opp, to_osib = (slab, sib), (slab, opp), (slab, osib)
    to_high, to_back = ((slab + 32) % 64, m), ((slab + 32) % 64, opp)
    peers = [to_sib, to_opp, to_osib, to_high, to_back]
    peers += [at_slab(k) for k in (-4, -3, -2, -1, 1, 2, 3, 4)]
    peers += [at_x(k) for k in range(1, 4)] + [at_z(k) for k in range(1, 8)]
    peers += [at_high_x(k) for k in range(1, 4)]
    sent = []

    class Send:
        def __init__(self, src, dst, device, leaves=None, comes=None):
            i = len(sent)
            self.copy = pltpu.make_async_remote_copy(
                src_ref=src, dst_ref=dst, send_sem=ssem.at[i], recv_sem=rsem.at[i],
                device_id=device, device_id_type=MESH,
            )
            self.leaves, self.comes = leaves, comes
            self.act(leaves, self.copy.start)
            sent.append(self)

        def act(self, condition, action):
            if condition is None:
                action()
            else:
                pl.when(condition)(action)

        def wait_recv(self):
            self.act(self.comes, self.copy.wait_recv)

        def wait_send(self):
            self.act(self.leaves, self.copy.wait_send)

    def near_slab(src, dst, distance):
        return Send(src, dst, at_slab(distance), inside(distance), inside(-distance))

    def rows(count, index):
        return pl.ds(pl.multiple_of(count * index, count), count)

    loads = [
        pltpu.make_async_copy(src, dst, lsem.at[i])
        for i, (src, dst) in enumerate((
            (q_hbm, q_ref), (head_hbm, head.at[rows(256, m)]), (p_hbm, p_ref),
            (mask_hbm, mask_ref), (counts_hbm, counts_ref), (pos_hbm, pos_ref),
            (weight_hbm, weight_ref),
        ))
    ]
    for copy in loads:
        copy.start()
    barrier = pltpu.get_barrier_semaphore()
    for peer in peers:
        pl.semaphore_signal(barrier, inc=1, device_id=peer, device_id_type=MESH)

    for k in (-4, -3, -2, -1, 1, 2, 3, 4):
        @pl.when(jnp.logical_not(inside(k)))
        def _():
            ttr[k + 4] = jnp.zeros((4, 128), F32)
            if abs(k) <= 2:
                qb[(2 + k) * QM : (3 + k) * QM] = jnp.zeros((QM, D), BF)
                if abs(k) == 1:
                    gr[k + 2] = jnp.zeros((QM, D), BF)
                auxr[k + 2] = jnp.zeros((8, 128), F32)

    for k in (1, -1):
        @pl.when(jnp.logical_not(jnp.logical_and(inside(k), inside(-k))))
        def _():
            gr[2 - 2 * k] = jnp.zeros((QM, D), BF)

    loads[0].wait()
    loads[1].wait()
    own_head = head[rows(256, m)]
    part_q[...] = jnp.dot(q_ref[...], own_head, preferred_element_type=F32).astype(BF)
    pl.semaphore_wait(barrier, len(peers))
    q1 = Send(part_q.at[rows(QM, osib)], rq.at[1], to_sib)
    q0 = Send(part_q.at[rows(QM, sib)], rq.at[0], to_sib)

    def head_rows(member, start, size):
        return head.at[pl.ds(pl.multiple_of(member * 256 + start, 32), size)]

    half_mine, half_other = 128 * (xi % 2), 128 * (1 - xi % 2)
    heads = []
    for j in range(4):
        mine = head_rows(m, half_mine + 32 * j, 32)
        heads.append(Send(mine, mine, to_back))
    near_head = Send(head_rows(m, 0, 256), head_rows(m, 0, 256), to_sib)
    q1.wait_recv()
    yq[...] = (part_q[rows(QM, opp)].astype(F32) + rq[1].astype(F32)).astype(BF)
    q2 = Send(yq, zq, to_opp)

    loads[2].wait()
    feature = rows(256, m)
    wide = [
        Send(p_ref.at[rows(256, core)], xh.at[:, feature], to_opp),
        Send(p_ref.at[rows(256, 1 - core)], xh.at[:, feature], to_osib),
        Send(p_ref.at[rows(256, 1 - core)], xh.at[:, feature], to_sib),
    ]
    xh[:, feature] = p_ref[rows(256, core)]
    side_heads, far_heads = [], []

    def pass_head(j):
        heads[j].wait_recv()
        theirs = head_rows(opp, half_mine + 32 * j, 32)
        side_heads.append(Send(theirs, theirs, at_x(1 if j % 2 == 0 else 3)))
        far_heads.append(Send(theirs, theirs, to_sib))


    def own_lanes(value):
        quarters = [value[:, k * QM : (k + 1) * QM] for k in range(4)]
        return jnp.where(
            m == 0, quarters[0],
            jnp.where(m == 1, quarters[1], jnp.where(m == 2, quarters[2], quarters[3])),
        )

    for copy in loads[3:]:
        copy.wait()
    count = counts_ref[slab]
    count_f = count.astype(F32)
    weight = own_lanes(weight_ref[...])
    slot = own_lanes(pos_ref[...].astype(F32))
    wanted = slot - count_f * jnp.floor((slot + 0.5) / count_f)
    auxs[...] = jnp.zeros_like(auxs)
    for k in range(5):
        auxs[k, 0:4, 0:QM] = own_lanes(mask_ref[k].astype(F32))
        auxs[k, 4:5, 0:QM] = weight
    xo[0:QM, rows(256, low)] = q_ref[rows(QM, m)]
    xo[QM:192, rows(256, low)] = p_ref[rows(PM, p_own)]
    xo[192 : 192 + QM, rows(256, low)] = q_ref[rows(QM, sib)]
    xo[192 + QM :, rows(256, low)] = p_ref[rows(PM, p_sib)]

    def normalise(projected):
        norm = jnp.sqrt(jnp.sum(projected * projected, axis=1, keepdims=True) + EPS)
        return projected / norm, norm

    pass_head(0)
    pass_head(1)
    q0.wait_recv()
    q2.wait_recv()
    unit, norm = normalise(
        part_q[rows(QM, m)].astype(F32) + rq[0].astype(F32) + zq[...].astype(F32)
    )
    unit_q[...] = unit
    norm_q[...] = norm
    qb[2 * QM : 3 * QM] = unit.astype(BF)
    halves = [slice(0, 32), slice(32, 64)]

    def query_piece(k, h):
        return qb.at[(2 - k) * QM + h * 32 : (2 - k) * QM + (h + 1) * 32]

    queries, auxes = [], []
    for h in range(2):
        for k in (1, -1):
            queries.append(near_slab(query_piece(0, h), query_piece(k, h), k))
    for k in (1, -1, 2, -2):
        auxes.append(near_slab(auxs.at[2 + k], auxr.at[2 - k], k))

    def pass_on(h):
        for i, k in enumerate((1, -1)):
            queries[2 * h + i].wait_recv()
            further.append(
                Send(
                    query_piece(k, h), query_piece(2 * k, h), at_slab(k),
                    jnp.logical_and(inside(k), inside(-k)), inside(-2 * k),
                )
            )

    further = []
    pass_head(2)
    pass_head(3)
    wide_q = [
        Send(q_ref.at[rows(QM, member)], xo.at[first : first + QM, rows(256, low)], to_opp)
        for first, member in ((0, opp), (192, osib))
    ]

    def chip_part(chip):
        features = rows(512, chip)
        return jnp.dot(xh[:, features], head[features], preferred_element_type=F32)

    wide[2].wait_recv()
    near_head.wait_recv()
    projected = chip_part(low)
    for j in range(4):
        side_heads[j].wait_recv()
        theirs = head_rows(opp, half_other + 32 * j, 32)
        far_heads.append(Send(theirs, theirs, to_sib))
        if j % 2 == 1:
            pass_on(j // 2)
    for copy in wide[:2] + far_heads:
        copy.wait_recv()
    unit, norm = normalise(projected + chip_part(1 - low))
    unit_p[...] = unit
    norm_p[...] = norm
    pb[rows(256, core)] = unit.astype(BF)
    mine = pb.at[rows(256, core)]
    near = Send(mine, mine, to_sib)
    xo[QM:192, rows(256, 1 - low)] = xh[rows(PM, low), rows(256, opp)]
    wide_q.append(
        Send(xh.at[rows(PM, low), rows(256, osib)], xo.at[192 + QM : 384, rows(256, 1 - low)], to_sib)
    )
    near.wait_recv()
    for copy in further + auxes:
        copy.wait_recv()

    auxr[2] = auxs[2]
    for k in range(5):
        lanes = slice(k * QM, (k + 1) * QM)
        auxc[:, lanes] = auxr[k][:, 0:QM]
        auxc[5:6, lanes] = wanted if k == 2 else jnp.full((1, QM), -1.0, F32)
    scores = lax.dot_general(
        pb[...], qb[...], (((1,), (1,)), ((), ())), preferred_element_type=F32
    )
    slot_ids = lax.broadcasted_iota(jnp.int32, (PM, NQ), 0)
    others = jnp.zeros((1, NQ), F32)
    positive = jnp.zeros((1, NQ), F32)
    for tile in range(4):
        ids = slot_ids + tile * PM
        is_positive = ids.astype(F32) == auxc[5:6, :]
        kept = (ids < count) & (auxc[tile : tile + 1, :] > 0.5) & jnp.logical_not(is_positive)
        grown = jnp.exp(scores[tile * PM : (tile + 1) * PM] / TAU)
        terms = jnp.where(kept, grown, 0.0)
        others = others + jnp.sum(terms, axis=0, keepdims=True)
        positive = positive + jnp.sum(jnp.where(is_positive, grown, 0.0), axis=0, keepdims=True)
        ef[tile * PM : (tile + 1) * PM] = terms
        eb[tile * PM : (tile + 1) * PM] = terms.astype(BF)
    for k in range(5):
        tts[k // 2 : k // 2 + 1, (k % 2) * QM : (k % 2 + 1) * QM] = others[
            :, k * QM : (k + 1) * QM
        ]
    tts[2:3, QM:128] = positive[:, 2 * QM : 3 * QM]
    tts[3:4, :] = jnp.zeros((1, 128), F32)
    totals = [near_slab(tts, ttr.at[4 - k], k) for k in (1, -1, 2, -2, 3, -3, 4, -4)]

    terms = lax.dot_general(
        eb[...], pb[...], (((0,), (0,)), ((), ())), preferred_element_type=F32
    )
    relay = []
    for h in range(2):
        for k in (1, -1):
            lines = slice((2 + 2 * k) * QM + 32 * h, (2 + 2 * k) * QM + 32 * (h + 1))
            gs[2 + 2 * k, halves[h]] = terms[lines].astype(BF)
            relay.append(
                Send(
                    gs.at[2 + 2 * k, halves[h]], gr.at[2 - 2 * k, halves[h]], at_slab(k),
                    jnp.logical_and(inside(k), inside(2 * k)),
                    jnp.logical_and(inside(k), inside(-k)),
                )
            )
    own_terms = terms[2 * QM : 3 * QM]
    nearest = {k: terms[(2 + k) * QM : (3 + k) * QM] for k in (1, -1)}
    returns = []

    def add_relayed(h):
        for i, k in enumerate((1, -1)):
            relay[2 * h + i].wait_recv()
            gs[2 + k, halves[h]] = (
                nearest[k][halves[h]] + gr[2 - 2 * k, halves[h]].astype(F32)
            ).astype(BF)
            returns.append(
                near_slab(gs.at[2 + k, halves[h]], gr.at[2 - k, halves[h]], k)
            )


    ttr[4] = tts[...]
    for copy in totals:
        copy.wait_recv()
    for k in range(-2, 3):
        rest = jnp.zeros((1, QM), F32)
        for j in range(-2, 3):
            n = 2 - j
            rest = rest + ttr[k + j + 4][n // 2 : n // 2 + 1, (n % 2) * QM : (n % 2 + 1) * QM]
        whole = rest + ttr[k + 4][2:3, QM:128]
        lanes = slice((2 + k) * QM, (3 + k) * QM)
        scale = auxc[4:5, lanes] / (whole * TAU)
        auxc[6:7, lanes] = jnp.where(inside(k), scale, 0.0)
        if k == 0:
            own_rest, own_whole = rest, whole
            auxc[7:8, lanes] = scale * rest
        else:
            auxc[7:8, lanes] = jnp.zeros((1, QM), F32)

    def passage_terms(index):
        is_positive = (slot_ids + index * PM).astype(F32) == auxc[5:6, :]
        coefficient = jnp.where(is_positive, -auxc[7:8, :], ef[rows(PM, index)] * auxc[6:7, :])
        return jnp.dot(coefficient.astype(BF), qb[...], preferred_element_type=F32)

    pps[1] = passage_terms(p_osib).astype(BF)
    pieces = [slice(0, 64), slice(64, 128)]
    p1 = [Send(pps.at[1, piece], pr.at[1, piece], to_sib) for piece in pieces]
    part = passage_terms(p_opp)
    add_relayed(0)
    p2 = []
    for copy, piece in zip(p1, pieces):
        copy.wait_recv()
        py[piece] = (part[piece] + pr[1, piece].astype(F32)).astype(BF)
        p2.append(Send(py.at[piece], pz.at[piece], to_opp))
    add_relayed(1)
    pps[0] = passage_terms(p_sib).astype(BF)
    p0 = Send(pps.at[0], pr.at[0], to_sib)
    own_part = passage_terms(p_own)

    def tangent(unit, norm, grad):
        radial = jnp.sum(unit * grad, axis=1, keepdims=True)
        return ((grad - unit * radial) / norm).astype(BF)

    eye = lax.broadcasted_iota(jnp.int32, (QM, QM), 0) == lax.broadcasted_iota(
        jnp.int32, (QM, QM), 1
    )

    def column(row):
        return jnp.sum(jnp.where(eye, row, 0.0), axis=1, keepdims=True)

    one_hot = (
        lax.broadcasted_iota(jnp.int32, (4 * PM, QM), 0).astype(F32) == wanted
    ).astype(F32).astype(BF)
    chosen = lax.dot_general(
        one_hot, pb[...], (((0,), (0,)), ((), ())), preferred_element_type=F32
    )
    scale = column(weight / (own_whole * TAU))
    drop = column(weight * own_rest / (own_whole * TAU))
    for copy in returns:
        copy.wait_recv()
    for k in (1, 3):
        own_terms = own_terms + gr[k].astype(F32)
    pgt[0:QM] = tangent(unit_q[...], norm_q[...], own_terms * scale - chosen * drop)
    shared = [Send(pgt.at[0:QM], pgt.at[192 : 192 + QM], to_sib)]
    p0.wait_recv()
    for i, piece in enumerate(pieces):
        p2[i].wait_recv()
        there = slice(QM + 64 * i, QM + 64 * (i + 1))
        line = pl.ds(pl.multiple_of(PM * low + 64 * i, 64), 64)
        summed = own_part[piece] + pr[0, piece].astype(F32) + pz[piece].astype(F32)
        pgt[there] = tangent(unit_p[line], norm_p[line], summed)
        shared.append(
            Send(pgt.at[there], pgt.at[192 + QM + 64 * i : 192 + QM + 64 * (i + 1)], to_sib)
        )

    def cols(size, index):
        return pl.ds(pl.multiple_of(index * size, size), size)

    for copy in wide_q + shared:
        copy.wait_recv()

    first, second, third, fourth, last = ([[], []] for _ in range(5))

    def term(half):
        features = jnp.concatenate(
            [xo[:, k + half * 128 : k + (half + 1) * 128] for k in (0, 256)], axis=1
        )
        total = lax.dot_general(
            features, pgt[...], (((0,), (0,)), ((), ())), preferred_element_type=F32
        )
        there = slice(half * 128, (half + 1) * 128)
        for block in range(2):
            hf[block, there] = total[block * 128 : (block + 1) * 128]
            hb[block, there] = total[block * 128 : (block + 1) * 128].astype(BF)

    term(0)
    for s in range(2):
        there = slice(64 * s, 64 * (s + 1))
        for k in (2, 1, 3):
            first[s].append(
                Send(hb.at[:, there, cols(256, (xi + k) % 4)], ax.at[s, k - 1], at_x(k))
            )
    term(1)
    for s in range(2):
        there = slice(128 + 64 * s, 128 + 64 * (s + 1))
        first[s] += [
            Send(hb.at[low, there, cols(512, 1 - high)], cy.at[s, 2], to_high),
            Send(hb.at[1 - low, there, cols(512, high)], cy.at[s, 0], to_opp),
            Send(hb.at[1 - low, there, cols(512, 1 - high)], cy.at[s, 1], to_back),
        ]

    eo[...] = lax.dot_general(
        pgt[0:192], head[...], (((1,), (1,)), ((), ())), preferred_element_type=F32
    ).astype(BF)
    oq_ref[rows(QM, m)] = eo[0:QM, cols(256, m)]
    op_ref[rows(PM, p_own)] = eo[QM:, cols(256, m)]

    def spread(member, device):
        return [
            Send(eo.at[0:QM, cols(256, member)], oq_ref.at[rows(QM, m)], device),
            Send(eo.at[QM : QM + PM, cols(256, member)], op_ref.at[rows(PM, p_own)], device),
        ]

    outs = spread(sib, to_sib)

    def plus(total, ref, s, count):
        for k in range(count):
            total = total + ref[s, k].astype(F32)
        return total

    def along_second(s):
        for copy in first[s][:3]:
            copy.wait_recv()
        total = plus(hf[:, 64 * s : 64 * (s + 1), cols(256, xi)], ax, s, 3)
        a1f[s] = total
        a1[s] = total.astype(BF)
        second[s] += [
            Send(a1.at[s, low, :, cols(128, 1 - high)], ay.at[s, 2], to_high),
            Send(a1.at[s, 1 - low, :, cols(128, high)], ay.at[s, 0], to_opp),
            Send(a1.at[s, 1 - low, :, cols(128, 1 - high)], ay.at[s, 1], to_back),
        ]
        for copy in first[s][3:]:
            copy.wait_recv()
        total = plus(hf[low, 128 + 64 * s : 128 + 64 * (s + 1), cols(512, high)], cy, s, 3)
        c1f[s] = total
        c1[s] = total.astype(BF)
        for k in (2, 1, 3):
            second[s].append(
                Send(c1.at[s, :, cols(128, (xi + k) % 4)], cx.at[s, k - 1], at_x(k))
            )

    def along_z(s):
        for copy in second[s]:
            copy.wait_recv()
        total = plus(a1f[s, low, :, cols(128, high)], ay, s, 3)
        e1f[s, 0:64] = total
        e1[s, 0:64] = total.astype(BF)
        total = plus(c1f[s, :, cols(128, xi)], cx, s, 3)
        e1f[s, 64:128] = total
        e1[s, 64:128] = total.astype(BF)
        for k in (4, 3, 5, 2, 6, 1, 7):
            third[s].append(Send(e1.at[s, rows(16, (zi + k) % 8)], ez.at[s, k - 1], at_z(k)))

    def back_z(s):
        for copy in third[s]:
            copy.wait_recv()
        mine = gz.at[s, rows(16, zi)]
        mine[...] = plus(e1f[s, rows(16, zi)], ez, s, 7).astype(BF)
        for k in (4, 3, 5, 2, 6, 1, 7):
            fourth[s].append(Send(mine, mine, at_z(k)))

    own = high * 4 + xi

    def back(s):
        for copy in fourth[s]:
            copy.wait_recv()
        last[s] += [Send(gz.at[s], ga.at[s, own], at_high_x(k)) for k in (2, 1, 3)]
        last[s] += [Send(gz.at[s], ga.at[s, own], at_x(k)) for k in (2, 1, 3)]
        last[s].append(Send(gz.at[s], ga.at[s, own], to_high))
        ga[s, own] = gz[s]

    along_second(0)
    along_second(1)
    along_z(0)
    along_z(1)
    outs += spread(opp, to_opp) + spread(osib, to_osib)
    back_z(0)
    back_z(1)
    back(0)
    back(1)
    for s in range(2):
        for copy in last[s]:
            copy.wait_recv()
        for j in range(8):
            upper, lower = 128 * (2 * (j % 4) + j // 4), 128 * j
            oh_ref[64 * s : 64 * (s + 1), upper : upper + 128] = ga[s, j, 0:64]
            oh_ref[128 + 64 * s : 128 + 64 * (s + 1), lower : lower + 128] = ga[s, j, 64:128]
    for copy in outs:
        copy.wait_recv()
    for copy in sent:
        copy.wait_send()


def emit(query, passage, term, query_out, passage_out, head_out, wide, sems):
    copies = [
        pltpu.make_async_copy(query, query_out, sems.at[0]),
        pltpu.make_async_copy(passage, passage_out, sems.at[1]),
    ]
    for copy in copies:
        copy.start()
    for part in range(2):
        there = slice(part * 128, (part + 1) * 128)
        wide[there] = term[there].astype(F32)
        copies.append(
            pltpu.make_async_copy(wide.at[there], head_out.at[there], sems.at[2 + part])
        )
        copies[-1].start()
    for copy in copies:
        copy.wait()


def body(query_emb, passage_emb, head, fn_mask, counts, positive_slot, query_weight):
    vmem = pl.BlockSpec(memory_space=pltpu.VMEM)
    hbm = pl.BlockSpec(memory_space=pltpu.HBM)

    def half(*shape):
        return pltpu.VMEM(shape, BF)

    def full(*shape):
        return pltpu.VMEM(shape, F32)

    grads = pl.pallas_call(
        kernel,
        out_shape=(
            jax.ShapeDtypeStruct((256, 256), BF),
            jax.ShapeDtypeStruct((512, 256), BF),
            jax.ShapeDtypeStruct((256, D), BF),
        ),
        in_specs=[hbm] * 7,
        out_specs=(vmem, vmem, vmem),
        scratch_shapes=[
            half(256, 256), half(512, 256), half(D, D),
            pltpu.VMEM((5, 4, 256), jnp.int32), pltpu.SMEM((64,), jnp.int32),
            pltpu.VMEM((1, 256), jnp.int32), full(1, 256),
            half(256, D), half(2, QM, D), half(QM, D), half(QM, D), half(256, D),
            full(QM, D), full(256, D), full(QM, 1), full(256, 1),
            half(NQ, D), half(4 * PM, D), full(5, 8, 128), full(5, 8, 128), full(8, NQ),
            full(4 * PM, NQ), half(4 * PM, NQ), full(4, 128), full(9, 4, 128),
            half(5, QM, D), half(5, QM, D),
            half(2, PM, D), half(2, PM, D), half(PM, D), half(PM, D),
            half(384, 512), half(384, D), half(192, D),
            full(2, 256, D), half(2, 256, D),
            half(2, 3, 2, 64, 256), half(2, 3, 64, 512),
            full(2, 2, 64, 256), full(2, 64, 512), half(2, 2, 64, 256), half(2, 64, 512),
            half(2, 3, 64, 128), half(2, 3, 64, 128), full(2, 128, 128), half(2, 128, 128),
            half(2, 7, 16, 128), half(2, 128, 128), half(2, 8, 128, 128),
            pltpu.SemaphoreType.DMA((7,)),
            pltpu.SemaphoreType.DMA((SEMS,)), pltpu.SemaphoreType.DMA((SEMS,)),
        ],
        compiler_params=pltpu.CompilerParams(
            collective_id=0, has_side_effects=True, vmem_limit_bytes=48 << 20
        ),
        cost_estimate=pl.CostEstimate(flops=3 << 30, bytes_accessed=4 << 20, transcendentals=0),
    )(*[
        pltpu.with_memory_space_constraint(value, pltpu.HBM)
        for value in (
            query_emb, passage_emb, head, jnp.transpose(fn_mask, (1, 2, 0)), counts,
            positive_slot.reshape(1, -1), query_weight.reshape(1, -1),
        )
    ])
    return pl.pallas_call(
        emit,
        out_shape=(
            jax.ShapeDtypeStruct((256, 256), BF),
            jax.ShapeDtypeStruct((512, 256), BF),
            jax.ShapeDtypeStruct((256, D), F32),
        ),
        in_specs=[vmem] * 3,
        out_specs=(hbm,) * 3,
        scratch_shapes=[full(256, D), pltpu.SemaphoreType.DMA((4,))],
        compiler_params=pltpu.CompilerParams(vmem_limit_bytes=8 << 20),
    )(*grads)


def solution(mesh):
    return jax.shard_map(
        body,
        mesh=mesh,
        in_specs=(
            P("slab", "mp"), P("slab", "mp"), P("mp", None), P("slab", None, None),
            P(), P("slab"), P("slab"),
        ),
        out_specs=(P("slab", "mp"), P("slab", "mp"), P("mp", None)),
        check_vma=False,
    )
```

```python
import jax
import jax.numpy as jnp
from jax import lax
from jax.experimental import pallas as pl
from jax.experimental.pallas import tpu as pltpu
from jax.sharding import PartitionSpec as P

EPS = 1e-06
TAU = 0.05
D = 1024
QM = 64
PM = 128
NQ = 5 * QM
SEMS = 176
MESH = pl.DeviceIdType.MESH
BF = jnp.bfloat16
F32 = jnp.float32


def kernel(
    q_hbm, p_hbm, head_hbm, mask_hbm, counts_hbm, pos_hbm, weight_hbm,
    oq_ref, op_ref, oh_ref,
    q_ref, p_ref, head, mask_ref, counts_ref, pos_ref, weight_ref,
    part_q, rq, yq, zq, xh, unit_q, unit_p, norm_q, norm_p,
    qb, pb, auxs, auxr, auxc, ef, eb, tts, ttr, gs, gr,
    pps, pr, py, pz, xo, pgt, eo,
    hf, hb, ax, cy, a1f, c1f, a1, c1, ay, cx, e1f, e1, ez, gz, ga,
    lsem, ssem, rsem,
):
    slab = lax.axis_index("slab")
    m = lax.axis_index("mp")
    core, low = m % 2, m // 2
    sib = 2 * low + 1 - core
    opp = 2 * (1 - low) + core
    osib = 2 * (1 - low) + 1 - core
    high, xi, zi = slab // 32, (slab // 8) % 4, slab % 8
    p_own, p_sib = 2 * core + low, 2 * (1 - core) + low
    p_opp, p_osib = 2 * core + 1 - low, 2 * (1 - core) + 1 - low

    def at_slab(distance):
        there = (slab + distance + 64) % 64
        return (there, jnp.where(there // 32 == high, m, opp))

    def at_x(step):
        return (high * 32 + ((xi + step) % 4) * 8 + zi, m)

    def at_high_x(step):
        return ((1 - high) * 32 + ((xi + step) % 4) * 8 + zi, m)

    def at_z(step):
        return (high * 32 + xi * 8 + (zi + step) % 8, m)

    def inside(distance):
        return jnp.logical_and(slab + distance >= 0, slab + distance < 64)

    to_sib, to_opp, to_osib = (slab, sib), (slab, opp), (slab, osib)
    to_high, to_back = ((slab + 32) % 64, m), ((slab + 32) % 64, opp)
    peers = [to_sib, to_opp, to_osib, to_high, to_back]
    peers += [at_slab(k) for k in (-4, -3, -2, -1, 1, 2, 3, 4)]
    peers += [at_x(k) for k in range(1, 4)] + [at_z(k) for k in range(1, 8)]
    peers += [at_high_x(k) for k in range(1, 4)]
    sent = []

    class Send:
        def __init__(self, src, dst, device, leaves=None, comes=None):
            i = len(sent)
            self.copy = pltpu.make_async_remote_copy(
                src_ref=src, dst_ref=dst, send_sem=ssem.at[i], recv_sem=rsem.at[i],
                device_id=device, device_id_type=MESH,
            )
            self.leaves, self.comes = leaves, comes
            self.act(leaves, self.copy.start)
            sent.append(self)

        def act(self, condition, action):
            if condition is None:
                action()
            else:
                pl.when(condition)(action)

        def wait_recv(self):
            self.act(self.comes, self.copy.wait_recv)

        def wait_send(self):
            self.act(self.leaves, self.copy.wait_send)

    def near_slab(src, dst, distance):
        return Send(src, dst, at_slab(distance), inside(distance), inside(-distance))

    def rows(count, index):
        return pl.ds(pl.multiple_of(count * index, count), count)

    loads = [
        pltpu.make_async_copy(src, dst, lsem.at[i])
        for i, (src, dst) in enumerate((
            (q_hbm, q_ref), (head_hbm, head.at[rows(256, m)]), (p_hbm, p_ref),
            (mask_hbm, mask_ref), (counts_hbm, counts_ref), (pos_hbm, pos_ref),
            (weight_hbm, weight_ref),
        ))
    ]
    for copy in loads:
        copy.start()
    barrier = pltpu.get_barrier_semaphore()
    for peer in peers:
        pl.semaphore_signal(barrier, inc=1, device_id=peer, device_id_type=MESH)

    for k in (-4, -3, -2, -1, 1, 2, 3, 4):
        @pl.when(jnp.logical_not(inside(k)))
        def _():
            ttr[k + 4] = jnp.zeros((4, 128), F32)
            if abs(k) <= 2:
                qb[(2 + k) * QM : (3 + k) * QM] = jnp.zeros((QM, D), BF)
                if abs(k) == 1:
                    gr[k + 2] = jnp.zeros((QM, D), BF)
                auxr[k + 2] = jnp.zeros((8, 128), F32)

    for k in (1, -1):
        @pl.when(jnp.logical_not(jnp.logical_and(inside(k), inside(-k))))
        def _():
            gr[2 - 2 * k] = jnp.zeros((QM, D), BF)

    loads[0].wait()
    loads[1].wait()
    own_head = head[rows(256, m)]
    part_q[...] = jnp.dot(q_ref[...], own_head, preferred_element_type=F32).astype(BF)
    pl.semaphore_wait(barrier, len(peers))
    q1 = Send(part_q.at[rows(QM, osib)], rq.at[1], to_sib)
    q0 = Send(part_q.at[rows(QM, sib)], rq.at[0], to_sib)

    def head_rows(member, start, size):
        return head.at[pl.ds(pl.multiple_of(member * 256 + start, 32), size)]

    half_mine, half_other = 128 * (xi % 2), 128 * (1 - xi % 2)
    heads = []
    for j in range(4):
        mine = head_rows(m, half_mine + 32 * j, 32)
        heads.append(Send(mine, mine, to_back))
    near_head = Send(head_rows(m, 0, 256), head_rows(m, 0, 256), to_sib)
    q1.wait_recv()
    yq[...] = (part_q[rows(QM, opp)].astype(F32) + rq[1].astype(F32)).astype(BF)
    q2 = Send(yq, zq, to_opp)

    loads[2].wait()
    feature = rows(256, m)
    wide = [
        Send(p_ref.at[rows(256, core)], xh.at[:, feature], to_opp),
        Send(p_ref.at[rows(256, 1 - core)], xh.at[:, feature], to_osib),
        Send(p_ref.at[rows(256, 1 - core)], xh.at[:, feature], to_sib),
    ]
    xh[:, feature] = p_ref[rows(256, core)]
    side_heads, far_heads = [], []

    def pass_head(j):
        heads[j].wait_recv()
        theirs = head_rows(opp, half_mine + 32 * j, 32)
        side_heads.append(Send(theirs, theirs, at_x(1 if j % 2 == 0 else 3)))
        far_heads.append(Send(theirs, theirs, to_sib))


    def own_lanes(value):
        quarters = [value[:, k * QM : (k + 1) * QM] for k in range(4)]
        return jnp.where(
            m == 0, quarters[0],
            jnp.where(m == 1, quarters[1], jnp.where(m == 2, quarters[2], quarters[3])),
        )

    for copy in loads[3:]:
        copy.wait()
    count = counts_ref[slab]
    count_f = count.astype(F32)
    weight = own_lanes(weight_ref[...])
    slot = own_lanes(pos_ref[...].astype(F32))
    wanted = slot - count_f * jnp.floor((slot + 0.5) / count_f)
    auxs[...] = jnp.zeros_like(auxs)
    for k in range(5):
        auxs[k, 0:4, 0:QM] = own_lanes(mask_ref[k].astype(F32))
        auxs[k, 4:5, 0:QM] = weight
    xo[0:QM, rows(256, low)] = q_ref[rows(QM, m)]
    xo[QM:192, rows(256, low)] = p_ref[rows(PM, p_own)]
    xo[192 : 192 + QM, rows(256, low)] = q_ref[rows(QM, sib)]
    xo[192 + QM :, rows(256, low)] = p_ref[rows(PM, p_sib)]

    def normalise(projected):
        norm = jnp.sqrt(jnp.sum(projected * projected, axis=1, keepdims=True) + EPS)
        return projected / norm, norm

    pass_head(0)
    pass_head(1)
    q0.wait_recv()
    q2.wait_recv()
    unit, norm = normalise(
        part_q[rows(QM, m)].astype(F32) + rq[0].astype(F32) + zq[...].astype(F32)
    )
    unit_q[...] = unit
    norm_q[...] = norm
    qb[2 * QM : 3 * QM] = unit.astype(BF)
    halves = [slice(0, 32), slice(32, 64)]

    def query_piece(k, h):
        return qb.at[(2 - k) * QM + h * 32 : (2 - k) * QM + (h + 1) * 32]

    queries, auxes = [], []
    for h in range(2):
        for k in (1, -1):
            queries.append(near_slab(query_piece(0, h), query_piece(k, h), k))
    for k in (1, -1, 2, -2):
        auxes.append(near_slab(auxs.at[2 + k], auxr.at[2 - k], k))

    def pass_on(h):
        for i, k in enumerate((1, -1)):
            queries[2 * h + i].wait_recv()
            further.append(
                Send(
                    query_piece(k, h), query_piece(2 * k, h), at_slab(k),
                    jnp.logical_and(inside(k), inside(-k)), inside(-2 * k),
                )
            )

    further = []
    pass_head(2)
    pass_head(3)
    wide_q = [
        Send(q_ref.at[rows(QM, member)], xo.at[first : first + QM, rows(256, low)], to_opp)
        for first, member in ((0, opp), (192, osib))
    ]

    def chip_part(chip):
        features = rows(512, chip)
        return jnp.dot(xh[:, features], head[features], preferred_element_type=F32)

    wide[2].wait_recv()
    near_head.wait_recv()
    projected = chip_part(low)
    for j in range(4):
        side_heads[j].wait_recv()
        theirs = head_rows(opp, half_other + 32 * j, 32)
        far_heads.append(Send(theirs, theirs, to_sib))
        if j % 2 == 1:
            pass_on(j // 2)
    for copy in wide[:2] + far_heads:
        copy.wait_recv()
    unit, norm = normalise(projected + chip_part(1 - low))
    unit_p[...] = unit
    norm_p[...] = norm
    pb[rows(256, core)] = unit.astype(BF)
    mine = pb.at[rows(256, core)]
    near = Send(mine, mine, to_sib)
    xo[QM:192, rows(256, 1 - low)] = xh[rows(PM, low), rows(256, opp)]
    wide_q.append(
        Send(xh.at[rows(PM, low), rows(256, osib)], xo.at[192 + QM : 384, rows(256, 1 - low)], to_sib)
    )
    near.wait_recv()
    for copy in further + auxes:
        copy.wait_recv()

    auxr[2] = auxs[2]
    for k in range(5):
        lanes = slice(k * QM, (k + 1) * QM)
        auxc[:, lanes] = auxr[k][:, 0:QM]
        auxc[5:6, lanes] = wanted if k == 2 else jnp.full((1, QM), -1.0, F32)
    scores = lax.dot_general(
        pb[...], qb[...], (((1,), (1,)), ((), ())), preferred_element_type=F32
    )
    slot_ids = lax.broadcasted_iota(jnp.int32, (PM, NQ), 0)
    others = jnp.zeros((1, NQ), F32)
    positive = jnp.zeros((1, NQ), F32)
    for tile in range(4):
        ids = slot_ids + tile * PM
        is_positive = ids.astype(F32) == auxc[5:6, :]
        kept = (ids < count) & (auxc[tile : tile + 1, :] > 0.5) & jnp.logical_not(is_positive)
        grown = jnp.exp(scores[tile * PM : (tile + 1) * PM] / TAU)
        terms = jnp.where(kept, grown, 0.0)
        others = others + jnp.sum(terms, axis=0, keepdims=True)
        positive = positive + jnp.sum(jnp.where(is_positive, grown, 0.0), axis=0, keepdims=True)
        ef[tile * PM : (tile + 1) * PM] = terms
        eb[tile * PM : (tile + 1) * PM] = terms.astype(BF)
    for k in range(5):
        tts[k // 2 : k // 2 + 1, (k % 2) * QM : (k % 2 + 1) * QM] = others[
            :, k * QM : (k + 1) * QM
        ]
    tts[2:3, QM:128] = positive[:, 2 * QM : 3 * QM]
    tts[3:4, :] = jnp.zeros((1, 128), F32)
    totals = [near_slab(tts, ttr.at[4 - k], k) for k in (1, -1, 2, -2, 3, -3, 4, -4)]

    terms = lax.dot_general(
        eb[...], pb[...], (((0,), (0,)), ((), ())), preferred_element_type=F32
    )
    relay = []
    for h in range(2):
        for k in (1, -1):
            lines = slice((2 + 2 * k) * QM + 32 * h, (2 + 2 * k) * QM + 32 * (h + 1))
            gs[2 + 2 * k, halves[h]] = terms[lines].astype(BF)
            relay.append(
                Send(
                    gs.at[2 + 2 * k, halves[h]], gr.at[2 - 2 * k, halves[h]], at_slab(k),
                    jnp.logical_and(inside(k), inside(2 * k)),
                    jnp.logical_and(inside(k), inside(-k)),
                )
            )
    own_terms = terms[2 * QM : 3 * QM]
    nearest = {k: terms[(2 + k) * QM : (3 + k) * QM] for k in (1, -1)}
    returns = []

    def add_relayed(h):
        for i, k in enumerate((1, -1)):
            relay[2 * h + i].wait_recv()
            gs[2 + k, halves[h]] = (
                nearest[k][halves[h]] + gr[2 - 2 * k, halves[h]].astype(F32)
            ).astype(BF)
            returns.append(
                near_slab(gs.at[2 + k, halves[h]], gr.at[2 - k, halves[h]], k)
            )


    ttr[4] = tts[...]
    for copy in totals:
        copy.wait_recv()
    for k in range(-2, 3):
        rest = jnp.zeros((1, QM), F32)
        for j in range(-2, 3):
            n = 2 - j
            rest = rest + ttr[k + j + 4][n // 2 : n // 2 + 1, (n % 2) * QM : (n % 2 + 1) * QM]
        whole = rest + ttr[k + 4][2:3, QM:128]
        lanes = slice((2 + k) * QM, (3 + k) * QM)
        scale = auxc[4:5, lanes] / (whole * TAU)
        auxc[6:7, lanes] = jnp.where(inside(k), scale, 0.0)
        if k == 0:
            own_rest, own_whole = rest, whole
            auxc[7:8, lanes] = scale * rest
        else:
            auxc[7:8, lanes] = jnp.zeros((1, QM), F32)

    def coefficients(index):
        is_positive = (slot_ids + index * PM).astype(F32) == auxc[5:6, :]
        value = jnp.where(is_positive, -auxc[7:8, :], ef[rows(PM, index)] * auxc[6:7, :])
        return value.astype(BF)

    def passage_terms(*indices):
        value = jnp.concatenate([coefficients(index) for index in indices], axis=0)
        return jnp.dot(value, qb[...], preferred_element_type=F32)

    both = passage_terms(p_osib, p_opp)
    pps[1] = both[0:PM].astype(BF)
    pieces = [slice(0, 64), slice(64, 128)]
    p1 = [Send(pps.at[1, piece], pr.at[1, piece], to_sib) for piece in pieces]
    part = both[PM:]
    add_relayed(0)
    p2 = []
    for copy, piece in zip(p1, pieces):
        copy.wait_recv()
        py[piece] = (part[piece] + pr[1, piece].astype(F32)).astype(BF)
        p2.append(Send(py.at[piece], pz.at[piece], to_opp))
    add_relayed(1)
    both = passage_terms(p_sib, p_own)
    pps[0] = both[0:PM].astype(BF)
    p0 = Send(pps.at[0], pr.at[0], to_sib)
    own_part = both[PM:]

    def tangent(unit, norm, grad):
        radial = jnp.sum(unit * grad, axis=1, keepdims=True)
        return ((grad - unit * radial) / norm).astype(BF)

    eye = lax.broadcasted_iota(jnp.int32, (QM, QM), 0) == lax.broadcasted_iota(
        jnp.int32, (QM, QM), 1
    )

    def column(row):
        return jnp.sum(jnp.where(eye, row, 0.0), axis=1, keepdims=True)

    one_hot = (
        lax.broadcasted_iota(jnp.int32, (4 * PM, QM), 0).astype(F32) == wanted
    ).astype(F32).astype(BF)
    chosen = lax.dot_general(
        one_hot, pb[...], (((0,), (0,)), ((), ())), preferred_element_type=F32
    )
    scale = column(weight / (own_whole * TAU))
    drop = column(weight * own_rest / (own_whole * TAU))
    for copy in returns:
        copy.wait_recv()
    for k in (1, 3):
        own_terms = own_terms + gr[k].astype(F32)
    pgt[0:QM] = tangent(unit_q[...], norm_q[...], own_terms * scale - chosen * drop)
    shared = [Send(pgt.at[0:QM], pgt.at[192 : 192 + QM], to_sib)]
    p0.wait_recv()
    for i, piece in enumerate(pieces):
        p2[i].wait_recv()
        there = slice(QM + 64 * i, QM + 64 * (i + 1))
        line = pl.ds(pl.multiple_of(PM * low + 64 * i, 64), 64)
        summed = own_part[piece] + pr[0, piece].astype(F32) + pz[piece].astype(F32)
        pgt[there] = tangent(unit_p[line], norm_p[line], summed)
        shared.append(
            Send(pgt.at[there], pgt.at[192 + QM + 64 * i : 192 + QM + 64 * (i + 1)], to_sib)
        )

    def cols(size, index):
        return pl.ds(pl.multiple_of(index * size, size), size)

    for copy in wide_q + shared:
        copy.wait_recv()

    first, second, third, fourth, last = ([[], []] for _ in range(5))

    def term(half):
        features = jnp.concatenate(
            [xo[:, k + half * 128 : k + (half + 1) * 128] for k in (0, 256)], axis=1
        )
        total = lax.dot_general(
            features, pgt[...], (((0,), (0,)), ((), ())), preferred_element_type=F32
        )
        there = slice(half * 128, (half + 1) * 128)
        for block in range(2):
            hf[block, there] = total[block * 128 : (block + 1) * 128]
            hb[block, there] = total[block * 128 : (block + 1) * 128].astype(BF)

    term(0)
    for s in range(2):
        there = slice(64 * s, 64 * (s + 1))
        for k in (2, 1, 3):
            first[s].append(
                Send(hb.at[:, there, cols(256, (xi + k) % 4)], ax.at[s, k - 1], at_x(k))
            )
    term(1)
    for s in range(2):
        there = slice(128 + 64 * s, 128 + 64 * (s + 1))
        first[s] += [
            Send(hb.at[low, there, cols(512, 1 - high)], cy.at[s, 2], to_high),
            Send(hb.at[1 - low, there, cols(512, high)], cy.at[s, 0], to_opp),
            Send(hb.at[1 - low, there, cols(512, 1 - high)], cy.at[s, 1], to_back),
        ]

    eo[...] = lax.dot_general(
        pgt[0:192], head[...], (((1,), (1,)), ((), ())), preferred_element_type=F32
    ).astype(BF)
    oq_ref[rows(QM, m)] = eo[0:QM, cols(256, m)]
    op_ref[rows(PM, p_own)] = eo[QM:, cols(256, m)]

    def spread(member, device):
        return [
            Send(eo.at[0:QM, cols(256, member)], oq_ref.at[rows(QM, m)], device),
            Send(eo.at[QM : QM + PM, cols(256, member)], op_ref.at[rows(PM, p_own)], device),
        ]

    outs = spread(sib, to_sib)

    def plus(total, ref, s, count):
        for k in range(count):
            total = total + ref[s, k].astype(F32)
        return total

    def along_second(s):
        for copy in first[s][:3]:
            copy.wait_recv()
        total = plus(hf[:, 64 * s : 64 * (s + 1), cols(256, xi)], ax, s, 3)
        a1f[s] = total
        a1[s] = total.astype(BF)
        second[s] += [
            Send(a1.at[s, low, :, cols(128, 1 - high)], ay.at[s, 2], to_high),
            Send(a1.at[s, 1 - low, :, cols(128, high)], ay.at[s, 0], to_opp),
            Send(a1.at[s, 1 - low, :, cols(128, 1 - high)], ay.at[s, 1], to_back),
        ]
        for copy in first[s][3:]:
            copy.wait_recv()
        total = plus(hf[low, 128 + 64 * s : 128 + 64 * (s + 1), cols(512, high)], cy, s, 3)
        c1f[s] = total
        c1[s] = total.astype(BF)
        for k in (2, 1, 3):
            second[s].append(
                Send(c1.at[s, :, cols(128, (xi + k) % 4)], cx.at[s, k - 1], at_x(k))
            )

    def along_z(s):
        for copy in second[s]:
            copy.wait_recv()
        total = plus(a1f[s, low, :, cols(128, high)], ay, s, 3)
        e1f[s, 0:64] = total
        e1[s, 0:64] = total.astype(BF)
        total = plus(c1f[s, :, cols(128, xi)], cx, s, 3)
        e1f[s, 64:128] = total
        e1[s, 64:128] = total.astype(BF)
        for k in (4, 3, 5, 2, 6, 1, 7):
            third[s].append(Send(e1.at[s, rows(16, (zi + k) % 8)], ez.at[s, k - 1], at_z(k)))

    def back_z(s):
        for copy in third[s]:
            copy.wait_recv()
        mine = gz.at[s, rows(16, zi)]
        mine[...] = plus(e1f[s, rows(16, zi)], ez, s, 7).astype(BF)
        for k in (4, 3, 5, 2, 6, 1, 7):
            fourth[s].append(Send(mine, mine, at_z(k)))

    own = high * 4 + xi

    def back(s):
        for copy in fourth[s]:
            copy.wait_recv()
        last[s] += [Send(gz.at[s], ga.at[s, own], at_high_x(k)) for k in (2, 1, 3)]
        last[s] += [Send(gz.at[s], ga.at[s, own], at_x(k)) for k in (2, 1, 3)]
        last[s].append(Send(gz.at[s], ga.at[s, own], to_high))
        ga[s, own] = gz[s]

    along_second(0)
    along_second(1)
    along_z(0)
    along_z(1)
    outs += spread(opp, to_opp) + spread(osib, to_osib)
    back_z(0)
    back_z(1)
    back(0)
    back(1)
    for s in range(2):
        for copy in last[s]:
            copy.wait_recv()
        for j in range(8):
            upper, lower = 128 * (2 * (j % 4) + j // 4), 128 * j
            oh_ref[64 * s : 64 * (s + 1), upper : upper + 128] = ga[s, j, 0:64]
            oh_ref[128 + 64 * s : 128 + 64 * (s + 1), lower : lower + 128] = ga[s, j, 64:128]
    for copy in outs:
        copy.wait_recv()
    for copy in sent:
        copy.wait_send()


def emit(query, passage, term, query_out, passage_out, head_out, wide, sems):
    copies = [
        pltpu.make_async_copy(query, query_out, sems.at[0]),
        pltpu.make_async_copy(passage, passage_out, sems.at[1]),
    ]
    for copy in copies:
        copy.start()
    for part in range(2):
        there = slice(part * 128, (part + 1) * 128)
        wide[there] = term[there].astype(F32)
        copies.append(
            pltpu.make_async_copy(wide.at[there], head_out.at[there], sems.at[2 + part])
        )
        copies[-1].start()
    for copy in copies:
        copy.wait()


def body(query_emb, passage_emb, head, fn_mask, counts, positive_slot, query_weight):
    vmem = pl.BlockSpec(memory_space=pltpu.VMEM)
    hbm = pl.BlockSpec(memory_space=pltpu.HBM)

    def half(*shape):
        return pltpu.VMEM(shape, BF)

    def full(*shape):
        return pltpu.VMEM(shape, F32)

    grads = pl.pallas_call(
        kernel,
        out_shape=(
            jax.ShapeDtypeStruct((256, 256), BF),
            jax.ShapeDtypeStruct((512, 256), BF),
            jax.ShapeDtypeStruct((256, D), BF),
        ),
        in_specs=[hbm] * 7,
        out_specs=(vmem, vmem, vmem),
        scratch_shapes=[
            half(256, 256), half(512, 256), half(D, D),
            pltpu.VMEM((5, 4, 256), jnp.int32), pltpu.SMEM((64,), jnp.int32),
            pltpu.VMEM((1, 256), jnp.int32), full(1, 256),
            half(256, D), half(2, QM, D), half(QM, D), half(QM, D), half(256, D),
            full(QM, D), full(256, D), full(QM, 1), full(256, 1),
            half(NQ, D), half(4 * PM, D), full(5, 8, 128), full(5, 8, 128), full(8, NQ),
            full(4 * PM, NQ), half(4 * PM, NQ), full(4, 128), full(9, 4, 128),
            half(5, QM, D), half(5, QM, D),
            half(2, PM, D), half(2, PM, D), half(PM, D), half(PM, D),
            half(384, 512), half(384, D), half(192, D),
            full(2, 256, D), half(2, 256, D),
            half(2, 3, 2, 64, 256), half(2, 3, 64, 512),
            full(2, 2, 64, 256), full(2, 64, 512), half(2, 2, 64, 256), half(2, 64, 512),
            half(2, 3, 64, 128), half(2, 3, 64, 128), full(2, 128, 128), half(2, 128, 128),
            half(2, 7, 16, 128), half(2, 128, 128), half(2, 8, 128, 128),
            pltpu.SemaphoreType.DMA((7,)),
            pltpu.SemaphoreType.DMA((SEMS,)), pltpu.SemaphoreType.DMA((SEMS,)),
        ],
        compiler_params=pltpu.CompilerParams(
            collective_id=0, has_side_effects=True, vmem_limit_bytes=48 << 20
        ),
        cost_estimate=pl.CostEstimate(flops=3 << 30, bytes_accessed=4 << 20, transcendentals=0),
    )(*[
        pltpu.with_memory_space_constraint(value, pltpu.HBM)
        for value in (
            query_emb, passage_emb, head, jnp.transpose(fn_mask, (1, 2, 0)), counts,
            positive_slot.reshape(1, -1), query_weight.reshape(1, -1),
        )
    ])
    return pl.pallas_call(
        emit,
        out_shape=(
            jax.ShapeDtypeStruct((256, 256), BF),
            jax.ShapeDtypeStruct((512, 256), BF),
            jax.ShapeDtypeStruct((256, D), F32),
        ),
        in_specs=[vmem] * 3,
        out_specs=(hbm,) * 3,
        scratch_shapes=[full(256, D), pltpu.SemaphoreType.DMA((4,))],
        compiler_params=pltpu.CompilerParams(vmem_limit_bytes=8 << 20),
    )(*grads)


def solution(mesh):
    return jax.shard_map(
        body,
        mesh=mesh,
        in_specs=(
            P("slab", "mp"), P("slab", "mp"), P("mp", None), P("slab", None, None),
            P(), P("slab"), P("slab"),
        ),
        out_specs=(P("slab", "mp"), P("slab", "mp"), P("mp", None)),
        check_vma=False,
    )
```
